128 devices in a mesh: dp: 64 (over z, y, x), tp: 2 (over core).
Axes of the slice: x: 4, y: 4, z: 4, core: 2. Of those that a mesh axis runs over, the one named last changes fastest.
Arguments:
- moe_tokens: bfloat16 [8192, 3584], P('dp'), may hold values from -6 to 6
- slot_routes: int32 [8192, 8], P('dp'), may hold values from 0 to 127, all different within a row; in each aligned block of 128 rows (0 to 127, 128 to 255, ...) at most 10 rows name the same one
- route_gates: float32 [8192, 8], P('dp'), may hold values from 0.1 to 0.5
- w_in: bfloat16 [128, 3584, 1024], P('dp', None, 'tp'), may hold values from -0.09375 to 0.09375
- w_up: bfloat16 [128, 3584, 1024], P('dp', None, 'tp'), may hold values from -0.09375 to 0.09375
- w_out: bfloat16 [128, 1024, 3584], P('dp', 'tp'), may hold values from -0.1875 to 0.1875
- query_latent: bfloat16 [64, 128, 512], P('dp'), may hold values from -20 to 20
- query_rope: bfloat16 [64, 128, 64], P('dp'), may hold values from -4 to 4
- cache_latent: bfloat16 [64, 2048, 512], P('dp', 'tp'), may hold values from -5 to 5
- cache_rope: bfloat16 [64, 64, 2048], P('dp', None, 'tp'), may hold values from -4 to 4
- lengths: int32 [64], P('dp'), may hold values from 128 to 2048, as said below
Outputs:
- moe_out: bfloat16 [8192, 3584], P('dp', 'tp')
- attn_out: bfloat16 [64, 128, 512], P('dp')
The draws below stay inside these ranges and needn't reach their ends.
Inputs may be any that keep to these rules, and one draw needn't show every extreme that they name: `slot_routes`: each row names 8 different slots; within the rows of one dp index (aligned blocks of 128 rows) no slot is named more than 10 times, a bound that some block reaches. `lengths`: some row has all 2048 positions.
All inputs are finite; a program needn't handle non-finite values.
Results may differ from the reference program's by a relative error of at most 0.0057.
Values may be sent and summed in bfloat16 or wider, within the bound.
No kernel may reach another device: no remote copies, remote signals or barrier semaphores. Data moves between devices by JAX's collectives and lax.ppermute only.
A program may use at most 128 MiB of HBM per device.

```python
import math
import jax
import jax.numpy as jnp
import numpy as np
from jax import lax

D = 3584
H = 1024
HEADS = 128
LAT = 512
ROPE = 64
TOPK = 8
TOK_DEV = 128
CTX = 2048
ROWS = 64
TOKENS = 8192
SLOTS = 128
CAP = 10
N_DP = 64


def draw_cache_latent(key, part):
    key = jax.random.fold_in(key, 1)
    first = jax.random.fold_in(key, 0)
    values = jnp.clip(jax.random.normal(first, (ROWS, CTX, LAT), jnp.float32), -4.0, 4.0)
    return values.astype(jnp.bfloat16)


def draw_query_latent(key, part):
    key = jax.random.fold_in(key, 2)
    first = jax.random.fold_in(key, 0)
    values = jnp.clip(jax.random.normal(first, (ROWS, HEADS, LAT), jnp.float32), -4.0, 4.0)
    return values.astype(jnp.bfloat16)


def draw_lengths(key, part):
    key = jax.random.fold_in(key, 3)
    first, second = jax.random.split(key)
    values = jax.random.randint(first, (ROWS,), CTX // 16, CTX + 1, dtype=jnp.int32)
    longest = jax.random.randint(second, (), 0, ROWS, dtype=jnp.int32)
    return values.at[longest].set(CTX)


def shard_levels(key, extent, cuts, low, largest):
    def one(dim, blocks):
        steps = jax.random.uniform(jax.random.fold_in(jax.random.fold_in(key, 6), dim), (blocks,), jnp.float32, low / len(cuts), largest / len(cuts))
        return jnp.repeat(jnp.exp(steps), extent[dim] // blocks).reshape((-1,) + (1,) * (len(extent) - dim - 1))

    factor_of = one(*cuts[0])
    for cut in cuts[1:]:
        factor_of = factor_of * one(*cut)
    return factor_of


def deal_out(stream_key, own, number, rows, amount, top, bound, lean):
    order = jax.random.permutation(stream_key, amount)
    packed, common = load_shares(amount, rows * top, bound, lean, True), load_shares(amount, rows * top, bound, lean, False)
    places = jnp.arange(amount)

    def named(sizes, offset_by):
        used = int((sizes > 0).sum())
        fixed = max(1, used // 4)
        passed = fixed + (places - fixed + offset_by * (used - fixed)) % max(1, amount - fixed)
        return jnp.zeros((amount,), jnp.int32).at[order[jnp.where(places < fixed, places, passed)]].set(jnp.asarray(sizes, jnp.int32))

    sizes = jnp.where(number % 4 == 0, named(packed, number // 4), named(common, number - number // 4 - 1))
    mixed = jax.random.permutation(jax.random.fold_in(own, 3), amount)
    giver, taker = mixed[0:amount // 2 * 2:2], mixed[1:amount // 2 * 2:2]
    margin = jnp.minimum(sizes[giver] - 1, bound - sizes[taker]) // 2
    margin = jnp.where((giver == order[0]) | (taker == order[0]) | (sizes[taker] == 0), 0, jnp.maximum(margin, 0))
    passed = jax.random.randint(jax.random.fold_in(own, 4), (amount // 2,), 0, 1 << 20) % (margin + 1)
    sizes = sizes.at[giver].add(-passed).at[taker].add(passed)
    members = jnp.searchsorted(jnp.cumsum(sizes), jnp.arange(rows * top), side="right").astype(jnp.int32)
    listing = members.reshape(top, rows).T
    listing = listing[jax.random.permutation(jax.random.fold_in(own, 1), rows)]
    offset_by = jax.random.randint(jax.random.fold_in(own, 2), (rows, 1), 0, top)
    return jnp.take_along_axis(listing, (jnp.arange(top)[None, :] + offset_by) % top, axis=1)


def load_shares(count, total, most, skew, full):
    weights = [(1 << 20) // math.isqrt(standing ** skew) + 1 for standing in range(1, count + 1)]
    largest = most if full else min(most, max(-(-total // count), total * weights[0] // sum(weights)))
    least = 1 if total - largest >= count - 1 else 0
    counts, rest = [largest] + [least] * (count - 1), total - largest - least * (count - 1)
    while rest > 0:
        free = [i for i in range(1, count) if counts[i] < largest] or [i for i in range(1, count) if counts[i] < most]
        pool, remaining = sum([weights[i] for i in free]), rest
        for i in free:
            addition = min(most - counts[i], max(1, remaining * weights[i] // pool), rest)
            counts[i] = counts[i] + addition
            rest = rest - addition
    return np.array(counts)


def gaussian(own_key, extent, spread, bound, cuts=(), held_as=jnp.bfloat16):
    array = spread * jax.random.normal(own_key, extent, jnp.float32)
    if cuts:
        array = array * shard_levels(own_key, extent, cuts, -0.22, 0.18)
    return jnp.clip(array, -bound, bound).astype(held_as)


def setup_inputs(seed: int = 0) -> dict:
    keys = jax.random.split(jax.random.key(seed), 12)
    moe_tokens = gaussian(keys[0], (TOKENS, D), 1.0, 6.0, ((0, 64),))
    slot_routes_keys = jax.random.split(jax.random.fold_in(keys[1], 1), TOKENS // TOK_DEV)
    slot_routes_turns = jax.random.permutation(jax.random.fold_in(keys[1], 3), TOKENS // TOK_DEV)
    slot_routes = jax.vmap(lambda own, number: deal_out(jax.random.fold_in(keys[1], 2), own, number, TOK_DEV, SLOTS, TOPK, CAP, 2))(slot_routes_keys, slot_routes_turns).reshape((TOKENS, TOPK))
    route_gates = jnp.clip(0.1 + 0.4 * jax.random.uniform(keys[2], (TOKENS, TOPK), jnp.float32) ** shard_levels(keys[2], (TOKENS, TOPK), ((0, 64),), -0.2, 0.2), 0.1, 0.5)
    w_in = gaussian(keys[3], (SLOTS, D, H), D ** -0.5, 0.09375, ((0, 64), (2, 2)))
    w_up = gaussian(keys[4], (SLOTS, D, H), D ** -0.5, 0.09375, ((0, 64), (2, 2)))
    w_out = gaussian(keys[5], (SLOTS, H, D), H ** -0.5, 0.1875, ((0, 64), (1, 2)))
    query_latent = draw_query_latent(jax.random.fold_in(keys[11], 71), 0)
    query_rope = gaussian(keys[7], (ROWS, HEADS, ROPE), 1.0, 4.0, ((0, 64),))
    cache_latent = draw_cache_latent(jax.random.fold_in(keys[11], 71), 0)
    cache_rope = gaussian(keys[9], (ROWS, ROPE, CTX), 1.0, 4.0, ((0, 64), (2, 2)))
    lengths = draw_lengths(jax.random.fold_in(keys[11], 71), 0)
    return {"moe_tokens": moe_tokens, "slot_routes": slot_routes, "route_gates": route_gates, "w_in": w_in, "w_up": w_up, "w_out": w_out, "query_latent": query_latent, "query_rope": query_rope, "cache_latent": cache_latent, "cache_rope": cache_rope, "lengths": lengths}


softmax_scale = 192.0 ** -0.5 * (0.1 * math.log(40.0) + 1.0) ** 2


def attend_row(inputs):
    query_lat, query_rot, cache_lat, cache_rot, length = inputs
    scores = (jnp.dot(query_lat, cache_lat.T, preferred_element_type=jnp.float32) + jnp.dot(query_rot, cache_rot, preferred_element_type=jnp.float32)) * softmax_scale
    positions = jnp.arange(cache_lat.shape[0], dtype=jnp.int32)
    visible = positions[None, :] < length
    row_peak = jnp.max(jnp.where(visible, scores, -1e30), axis=1, keepdims=True)
    weights = jnp.where(visible, jnp.exp(scores - row_peak), 0.0)
    row_total = jnp.sum(weights, axis=1, keepdims=True)
    numerator = jnp.dot(weights.astype(jnp.bfloat16), cache_lat, preferred_element_type=jnp.float32)
    return (numerator / row_total).astype(jnp.bfloat16)


def routed_experts(moe_tokens, slot_routes, route_gates, w_in, w_up, w_out):
    route_slots = slot_routes.reshape(-1).astype(jnp.int32)
    route_tokens = jnp.arange(TOKENS * TOPK, dtype=jnp.int32) // TOPK
    route_weights = route_gates.reshape(-1)
    route_order = jnp.argsort(route_slots, stable=True).astype(jnp.int32)
    slot_ids = jnp.arange(SLOTS, dtype=jnp.int32)
    slot_loads = jnp.sum((route_slots[:, None] == slot_ids[None, :]).astype(jnp.int32), axis=0).astype(jnp.int32)
    slot_starts = (jnp.cumsum(slot_loads) - slot_loads).astype(jnp.int32)
    lane_index = jnp.arange(N_DP * CAP, dtype=jnp.int32)

    def serve_slot(accumulated, slot_index):
        occupied = lane_index < slot_loads[slot_index]
        sorted_place = jnp.where(occupied, slot_starts[slot_index] + lane_index, 0).astype(jnp.int32)
        routes = route_order[sorted_place]
        token_rows = route_tokens[routes]
        gate_values = jnp.where(occupied, route_weights[routes], 0.0)
        gathered = moe_tokens[token_rows]
        gate_part = jnp.dot(gathered, w_in[slot_index], preferred_element_type=jnp.float32)
        up_part = jnp.dot(gathered, w_up[slot_index], preferred_element_type=jnp.float32)
        hidden = (jax.nn.silu(gate_part) * up_part).astype(jnp.bfloat16)
        expert_out = jnp.dot(hidden, w_out[slot_index], preferred_element_type=jnp.float32).astype(jnp.bfloat16)
        accumulated = accumulated.at[token_rows].add(gate_values[:, None] * expert_out.astype(jnp.float32))
        return accumulated, None

    initial = jnp.zeros((TOKENS, moe_tokens.shape[1]), jnp.float32)
    combined, unused = lax.scan(serve_slot, initial, slot_ids)
    return combined.astype(jnp.bfloat16)


def reference(moe_tokens, slot_routes, route_gates, w_in, w_up, w_out, query_latent, query_rope, cache_latent, cache_rope, lengths):
    moe_out = routed_experts(moe_tokens, slot_routes, route_gates, w_in, w_up, w_out)
    attn_out = lax.map(attend_row, (query_latent, query_rope, cache_latent, cache_rope, lengths))
    return (moe_out, attn_out)
```

```python
import functools
import math

import jax
import jax.numpy as jnp
from jax import lax
from jax.experimental import pallas as pl
from jax.experimental.pallas import tpu as pltpu
from jax.sharding import PartitionSpec as P

softmax_scale = 192.0 ** (-0.5) * (0.1 * math.log(40.0) + 1.0) ** 2

GROUP = 512
BLOCK = 128
TILES = 5
MAIN = 8
REST = 2
CAP = 10
F32 = jnp.float32
BF16 = jnp.bfloat16
SWAP = ((0, 1), (1, 0))


def dot(a, b):
    return jnp.dot(a, b, preferred_element_type=F32)


def dot_nt(a, b):
    return lax.dot_general(a, b, (((1,), (1,)), ((), ())), preferred_element_type=F32)


def iota(shape, dim):
    return lax.broadcasted_iota(jnp.int32, shape, dim)


def rank_code(routes):
    tokens, top = routes.shape
    slots = iota((tokens, 128), 1)
    named = jnp.zeros((tokens, 128), F32)
    for k in range(top):
        named = named + (routes[:, k : k + 1] == slots).astype(F32)
    earlier = (iota((tokens, tokens), 1) < iota((tokens, tokens), 0)).astype(F32).astype(BF16)
    rank = dot(earlier, named.astype(BF16))
    return jnp.where(named > 0.0, rank, -1.0)


def dispatch_kernel(core_ref, routes_ref, tokens_ref, out_ref, main_ref, rest_ref):
    units = out_ref.shape[0] * MAIN

    @pl.when(pl.program_id(0) == 0)
    def _():
        code = rank_code(routes_ref[...]).astype(BF16)
        tokens = code.shape[0]
        unit = iota((units, 128), 0)
        owner = (iota((units, 128), 1) == 2 * (unit >> 3) + core_ref[0]).astype(F32).astype(BF16)
        spread = dot_nt(owner, code)
        unit = iota((units, tokens), 0)
        main_ref[...] = (spread == (unit & 7).astype(F32)).astype(F32).astype(BF16)
        rest = (spread == (MAIN + (unit & 1)).astype(F32)).astype(F32)
        block = (unit >> 1) & 3
        for f in range(4):
            rest_ref[:, f * tokens : (f + 1) * tokens] = jnp.where(block == f, rest, 0.0).astype(BF16)

    rows = tokens_ref[...]
    main = dot(main_ref[...], rows)
    for f in range(4):
        part = main[:, f * BLOCK : (f + 1) * BLOCK]
        out_ref[:, f] = part.reshape(-1, MAIN, BLOCK).astype(BF16)
    stacked = jnp.concatenate([rows[:, f * BLOCK : (f + 1) * BLOCK] for f in range(4)], axis=0)
    rest = dot(rest_ref[...], stacked)
    out_ref[:, 4] = rest.reshape(-1, MAIN, BLOCK).astype(BF16)


def dispatch(core, routes, tokens, dp_count):
    count, features = tokens.shape
    groups = features // GROUP
    units = dp_count * MAIN
    return pl.pallas_call(
        dispatch_kernel,
        grid=(groups,),
        in_specs=[
            pl.BlockSpec(memory_space=pltpu.SMEM),
            pl.BlockSpec(routes.shape, lambda g: (0, 0)),
            pl.BlockSpec((count, GROUP), lambda g: (0, g)),
        ],
        out_specs=pl.BlockSpec((dp_count, TILES, MAIN, BLOCK), lambda g: (0, g, 0, 0)),
        out_shape=jax.ShapeDtypeStruct((dp_count, TILES * groups, MAIN, BLOCK), BF16),
        scratch_shapes=[pltpu.VMEM((units, count), BF16), pltpu.VMEM((units, 4 * count), BF16)],
        compiler_params=pltpu.CompilerParams(vmem_limit_bytes=32 * 1024 * 1024),
        name="dispatch",
    )(core, routes, tokens)


def expert_kernel(
    core_ref,
    message_ref,
    in_own_ref,
    up_own_ref,
    in_far_ref,
    up_far_ref,
    out_own_ref,
    out_far_ref,
    back_ref,
    gate_acc,
    up_acc,
    hidden,
    pick,
    place,
):
    step = pl.program_id(0)
    groups = pl.num_programs(0) // 2
    units = message_ref.shape[0] * MAIN
    rest = message_ref.shape[0] * REST
    width = in_own_ref.shape[2]

    @pl.when(step == 0)
    def _():
        q, u = iota((4 * rest, units), 0), iota((4 * rest, units), 1)
        target = ((q & (rest - 1)) >> 1) * MAIN + (lax.div(q, rest)) * REST + (q & 1)
        pick[...] = (u == target).astype(F32).astype(BF16)
        u, q = iota((units, 4 * rest), 0), iota((units, 4 * rest), 1)
        target = ((q & (rest - 1)) >> 1) * MAIN + (lax.div(q, rest)) * REST + (q & 1)
        place[...] = (u == target).astype(F32).astype(BF16)
        gate_acc[...] = jnp.zeros_like(gate_acc)
        up_acc[...] = jnp.zeros_like(up_acc)

    @pl.when(step < groups)
    def _():
        main = jnp.concatenate(
            [message_ref[:, f].astype(F32).reshape(units, BLOCK).astype(BF16) for f in range(4)], axis=1
        )
        tail = message_ref[:, 4].astype(F32).reshape(units, BLOCK).astype(BF16)
        tail = dot(pick[...], tail).astype(BF16)
        tail = jnp.concatenate([tail[f * rest : (f + 1) * rest] for f in range(4)], axis=1)
        rows = jnp.concatenate([main, tail], axis=0)
        gate_acc[:, :width] += dot(rows, in_own_ref[0])
        up_acc[:, :width] += dot(rows, up_own_ref[0])
        gate_acc[:, width:] += dot(rows, in_far_ref[...])
        up_acc[:, width:] += dot(rows, up_far_ref[...])

    @pl.when(step == groups)
    def _():
        gate = gate_acc[...]
        hidden[...] = (gate / (1.0 + jnp.exp(-gate)) * up_acc[...]).astype(BF16)

    @pl.when(step >= groups)
    def _():
        value = dot(hidden[:, :width], out_own_ref[0]) + dot(hidden[:, width:], out_far_ref[...])
        for f in range(4):
            part = value[:units, f * BLOCK : (f + 1) * BLOCK]
            back_ref[:, f] = part.reshape(-1, MAIN, BLOCK).astype(BF16)
        tail = value[units:].astype(BF16)
        tail = jnp.concatenate([tail[:, f * BLOCK : (f + 1) * BLOCK] for f in range(4)], axis=0)
        back_ref[:, 4] = dot(place[...], tail).reshape(-1, MAIN, BLOCK).astype(BF16)


def experts(core, message, w_in, w_up, w_out, in_far, up_far, out_far):
    dp_count, tiles = message.shape[:2]
    groups = tiles // TILES
    width = w_in.shape[2]
    rows = dp_count * CAP
    units, rest = dp_count * MAIN, dp_count * REST

    def early(i):
        return jnp.minimum(i, groups - 1)

    def late(i):
        return jnp.maximum(i - groups, 0)

    return pl.pallas_call(
        expert_kernel,
        grid_spec=pltpu.PrefetchScalarGridSpec(
            num_scalar_prefetch=1,
            grid=(2 * groups,),
            in_specs=[
                pl.BlockSpec((dp_count, TILES, MAIN, BLOCK), lambda i, c: (0, early(i), 0, 0)),
                pl.BlockSpec((1, GROUP, width), lambda i, c: (c[0], early(i), 0)),
                pl.BlockSpec((1, GROUP, width), lambda i, c: (c[0], early(i), 0)),
                pl.BlockSpec((GROUP, width), lambda i, c: (early(i), 0)),
                pl.BlockSpec((GROUP, width), lambda i, c: (early(i), 0)),
                pl.BlockSpec((1, width, GROUP), lambda i, c: (c[0], 0, late(i))),
                pl.BlockSpec((width, GROUP), lambda i, c: (0, late(i))),
            ],
            out_specs=pl.BlockSpec((dp_count, TILES, MAIN, BLOCK), lambda i, c: (0, late(i), 0, 0)),
            scratch_shapes=[
                pltpu.VMEM((rows, 2 * width), F32),
                pltpu.VMEM((rows, 2 * width), F32),
                pltpu.VMEM((rows, 2 * width), BF16),
                pltpu.VMEM((4 * rest, units), BF16),
                pltpu.VMEM((units, 4 * rest), BF16),
            ],
        ),
        out_shape=jax.ShapeDtypeStruct(message.shape, BF16),
        compiler_params=pltpu.CompilerParams(vmem_limit_bytes=48 * 1024 * 1024),
        cost_estimate=pl.CostEstimate(
            flops=12 * rows * groups * GROUP * width, bytes_accessed=32 * 1024 * 1024, transcendentals=0
        ),
        name="experts",
    )(core, message, w_in, w_up, in_far, up_far, w_out, out_far)


def gates_kernel(core_ref, routes_ref, gates_ref, main_ref, rest_ref):
    routes, gates = routes_ref[...], gates_ref[...]
    tokens, top = routes.shape
    units = main_ref.shape[1]
    code = rank_code(routes).astype(BF16)
    slots = iota((tokens, 128), 1)
    value = jnp.zeros((tokens, 128), F32)
    for k in range(top):
        value = value + jnp.where(routes[:, k : k + 1] == slots, gates[:, k : k + 1], 0.0)
    high = value.astype(BF16)
    low = (value - high.astype(F32)).astype(BF16)
    unit = iota((128, units), 1)
    owner = (iota((128, units), 0) == 2 * (unit >> 3) + core_ref[0]).astype(F32).astype(BF16)
    spread = dot(code, owner)
    unit = iota((tokens, units), 1)
    block = (unit >> 1) & 3
    for part, source in enumerate((high, low)):
        gate = dot(source, owner)
        main = jnp.where(spread == (unit & 7).astype(F32), gate, 0.0)
        main_ref[part * tokens : (part + 1) * tokens] = main.astype(BF16)
        rest = jnp.where(spread == (MAIN + (unit & 1)).astype(F32), gate, 0.0)
        for f in range(4):
            at = (2 * f + part) * tokens
            rest_ref[at : at + tokens] = jnp.where(block == f, rest, 0.0).astype(BF16)


def spread_gates(core, routes, gates, dp_count):
    tokens = routes.shape[0]
    units = dp_count * MAIN
    whole = pl.BlockSpec(memory_space=pltpu.VMEM)
    return pl.pallas_call(
        gates_kernel,
        in_specs=[pl.BlockSpec(memory_space=pltpu.SMEM), whole, whole],
        out_specs=(whole, whole),
        out_shape=(
            jax.ShapeDtypeStruct((2 * tokens, units), BF16),
            jax.ShapeDtypeStruct((8 * tokens, units), BF16),
        ),
        compiler_params=pltpu.CompilerParams(vmem_limit_bytes=32 * 1024 * 1024),
        name="gates",
    )(core, routes, gates)


def combine_kernel(core_ref, back_ref, main_ref, rest_ref, keep_ref, send_ref):
    g = pl.program_id(0)
    units = main_ref.shape[1]
    tokens, half = keep_ref.shape
    blocks = half // BLOCK
    rows = jnp.concatenate(
        [back_ref[:, f].astype(F32).reshape(units, BLOCK).astype(BF16) for f in range(4)], axis=1
    )
    tail = back_ref[:, 4].astype(F32).reshape(units, BLOCK).astype(BF16)
    main = dot(main_ref[...], rows)
    rest = dot(rest_ref[...], tail)
    for f in range(4):
        lanes = slice(f * BLOCK, (f + 1) * BLOCK)
        at = 2 * f * tokens
        value = (
            main[:tokens, lanes]
            + main[tokens:, lanes]
            + rest[at : at + tokens]
            + rest[at + tokens : at + 2 * tokens]
        )
        index = 4 * g + f
        side = (index >= blocks).astype(jnp.int32)
        place = pl.ds(pl.multiple_of((index - side * blocks) * BLOCK, BLOCK), BLOCK)

        @pl.when(side == core_ref[0])
        def _():
            keep_ref[:, place] = value

        @pl.when(side != core_ref[0])
        def _():
            send_ref[:, place] = value


def combine(core, back, main, rest):
    dp_count, tiles = back.shape[:2]
    groups = tiles // TILES
    tokens, half = main.shape[0] // 2, groups * GROUP // 2
    out = jax.ShapeDtypeStruct((tokens, half), F32)
    return pl.pallas_call(
        combine_kernel,
        grid=(groups,),
        in_specs=[
            pl.BlockSpec(memory_space=pltpu.SMEM),
            pl.BlockSpec((dp_count, TILES, MAIN, BLOCK), lambda g: (0, g, 0, 0)),
            pl.BlockSpec(main.shape, lambda g: (0, 0)),
            pl.BlockSpec(rest.shape, lambda g: (0, 0)),
        ],
        out_specs=(pl.BlockSpec((tokens, half), lambda g: (0, 0)),) * 2,
        out_shape=(out, out),
        compiler_params=pltpu.CompilerParams(vmem_limit_bytes=32 * 1024 * 1024),
        name="combine",
    )(core, back, main, rest)


def attention(query_latent, query_rope, cache_latent, cache_rope, lengths):
    local_span = cache_latent.shape[1]
    positions = lax.axis_index("tp") * local_span + jnp.arange(local_span, dtype=jnp.int32)
    visible = positions[None, None, :] < lengths[:, None, None]
    scores = (
        jnp.einsum("bhl,btl->bht", query_latent, cache_latent, preferred_element_type=F32)
        + jnp.einsum("bhr,brt->bht", query_rope, cache_rope, preferred_element_type=F32)
    ) * softmax_scale
    peak = jnp.max(jnp.where(visible, scores, -1e30), axis=2, keepdims=True)
    weights = jnp.where(visible, jnp.exp(scores - peak), 0.0)
    total = jnp.sum(weights, axis=2, keepdims=True)
    numer = jnp.einsum("bht,btl->bhl", weights.astype(BF16), cache_latent, preferred_element_type=F32)
    both = jnp.concatenate(
        [numer, jnp.broadcast_to(total, total.shape[:2] + (64,)), jnp.broadcast_to(peak, peak.shape[:2] + (64,))],
        axis=2,
    )
    far = lax.ppermute(both, "tp", SWAP)
    lat = numer.shape[2]
    far_numer, far_total, far_peak = far[:, :, :lat], far[:, :, lat : lat + 1], far[:, :, lat + 64 : lat + 65]
    top = jnp.maximum(peak, far_peak)
    here, there = jnp.exp(peak - top), jnp.exp(far_peak - top)
    return ((numer * here + far_numer * there) / (total * here + far_total * there)).astype(BF16)


def body(
    moe_tokens,
    slot_routes,
    route_gates,
    w_in,
    w_up,
    w_out,
    query_latent,
    query_rope,
    cache_latent,
    cache_rope,
    lengths,
):
    dp_count = lax.axis_size("dp")
    index = lax.axis_index("tp")
    core = jnp.reshape(index, (1,)).astype(jnp.int32)
    outbound = dispatch(core, slot_routes, moe_tokens, dp_count)
    message = lax.all_to_all(outbound, "dp", split_axis=0, concat_axis=0, tiled=True)

    def swap(weight):
        return lax.ppermute(lax.dynamic_index_in_dim(weight, 1 - index, 0, False), "tp", SWAP)

    in_far, up_far, out_far = swap(w_in), swap(w_up), swap(w_out)
    gates_main, gates_rest = spread_gates(core, slot_routes, route_gates, dp_count)
    back = experts(core, message, w_in, w_up, w_out, in_far, up_far, out_far)
    returned = lax.all_to_all(back, "dp", split_axis=0, concat_axis=0, tiled=True)
    keep, send = combine(core, returned, gates_main, gates_rest)
    moe_out = (keep + lax.ppermute(send, "tp", SWAP)).astype(BF16)
    attn_out = attention(query_latent, query_rope, cache_latent, cache_rope, lengths)
    return (moe_out, attn_out)


def solution(mesh):
    placed = (
        P("dp", None),
        P("dp", None),
        P("dp", None),
        P("dp", None, "tp"),
        P("dp", None, "tp"),
        P("dp", "tp", None),
        P("dp", None, None),
        P("dp", None, None),
        P("dp", "tp", None),
        P("dp", None, "tp"),
        P("dp"),
    )
    return jax.shard_map(
        body,
        mesh=mesh,
        in_specs=placed,
        out_specs=(P("dp", "tp"), P("dp", None, None)),
        check_vma=False,
    )
```

```python
import math

import jax
import jax.numpy as jnp
from jax import lax
from jax.experimental import pallas as pl
from jax.experimental.pallas import tpu as pltpu
from jax.sharding import PartitionSpec as P

softmax_scale = 192.0 ** (-0.5) * (0.1 * math.log(40.0) + 1.0) ** 2

GROUP = 512
BLOCK = 128
TILES = 5
MAIN = 8
REST = 2
CAP = 10
F32 = jnp.float32
BF16 = jnp.bfloat16
SWAP = ((0, 1), (1, 0))
HBM = pl.BlockSpec(memory_space=pl.ANY)
VMEM = pl.BlockSpec(memory_space=pltpu.VMEM)
SMEM = pl.BlockSpec(memory_space=pltpu.SMEM)
PARAMS = pltpu.CompilerParams(vmem_limit_bytes=58 * 1024 * 1024)


def dot(a, b):
    return jnp.dot(a, b, preferred_element_type=F32)


def iota(shape, dim):
    return lax.broadcasted_iota(jnp.int32, shape, dim)


def one_hot(a, b):
    return (a == b).astype(F32).astype(BF16)


def tiles_of(ref, group):
    return ref.at[:, pl.ds(group * TILES, TILES)]


def features_of(group):
    return slice(group * GROUP, (group + 1) * GROUP)


def block_of(f):
    return slice(f * BLOCK, (f + 1) * BLOCK)


def unit_of(row, half):
    return ((row & (2 * half - 1)) >> 1) * MAIN + lax.div(row, 2 * half) * REST + (row & 1)


def fill_place(ref, dp_count):
    size = ref.shape[0]
    ref[...] = one_hot(iota((size, size), 0), unit_of(iota((size, size), 1), dp_count // 2))


def fill_pick(ref, dp_count):
    size = ref.shape[0]
    ref[...] = one_hot(iota((size, size), 1), unit_of(iota((size, size), 0), dp_count // 2))


def pack(value, place, ref, group):
    dp_count = ref.shape[0]
    main, half = dp_count * MAIN, dp_count // 2
    for f in range(4):
        ref[:, group * TILES + f] = value[:main, block_of(f)].astype(BF16).reshape(dp_count, MAIN, BLOCK)
    rest = value[main:].astype(BF16)
    sides = [rest[: 2 * half], rest[2 * half :]]
    sides = [jnp.concatenate([side[:, block_of(f)] for f in range(4)], axis=0) for side in sides]
    rest = dot(place, jnp.concatenate(sides, axis=1))
    for h in range(2):
        part = rest[:, block_of(h)].astype(BF16).reshape(half, MAIN, BLOCK)
        ref[h * half : (h + 1) * half, group * TILES + 4] = part


def unpack(ref, pick, group):
    dp_count = ref.shape[0]
    main, half = dp_count * MAIN, dp_count // 2
    rows = [ref[:, group * TILES + f].reshape(main, BLOCK) for f in range(4)]
    rest = ref[:, group * TILES + 4].reshape(main, BLOCK)
    rest = dot(pick, jnp.concatenate([rest[: main // 2], rest[main // 2 :]], axis=1)).astype(BF16)
    rest = [
        jnp.concatenate([rest[2 * half * f : 2 * half * (f + 1), block_of(h)] for f in range(4)], axis=1)
        for h in range(2)
    ]
    return jnp.concatenate([jnp.concatenate(rows, axis=1)] + rest, axis=0)


def row_of(index, dp_count):
    main = dp_count * MAIN
    first = index < main
    after = index - main
    return jnp.where(first, index >> 3, after >> 1), jnp.where(first, index & 7, MAIN + (after & 1))


def rank_code(routes):
    top, tokens = routes.shape
    slots = iota((128, tokens), 0)
    named = jnp.zeros((128, tokens), F32)
    for k in range(top):
        named = named + (routes[k : k + 1] == slots).astype(F32)
    earlier = (iota((tokens, tokens), 0) < iota((tokens, tokens), 1)).astype(F32).astype(BF16)
    rank = dot(named.astype(BF16), earlier)
    return jnp.where(named > 0.0, rank, -1.0)


def dispatch_kernel(core_ref, routes_ref, tokens_ref, out_ref, rows, chosen, place, packed, in_sem, out_sem):
    dp_count = out_ref.shape[0]
    groups = out_ref.shape[1] // TILES
    loads = [
        pltpu.make_async_copy(tokens_ref.at[:, features_of(g)], rows.at[:, features_of(g)], in_sem.at[g])
        for g in range(groups)
    ]
    stores = [
        pltpu.make_async_copy(tiles_of(packed, g), tiles_of(out_ref, g), out_sem.at[g]) for g in range(groups)
    ]
    for load in loads:
        load.start()
    fill_place(place, dp_count)
    code = rank_code(routes_ref[...]).astype(BF16)
    tokens = code.shape[1]
    count = dp_count * CAP
    owner, _ = row_of(iota((count, 128), 0), dp_count)
    spread = dot(one_hot(iota((count, 128), 1), 2 * owner + core_ref[0]), code)
    _, turn = row_of(iota((count, tokens), 0), dp_count)
    chosen[...] = one_hot(spread, turn.astype(F32))
    for g in range(groups):
        loads[g].wait()
        pack(dot(chosen[...], rows[:, features_of(g)]), place[...], packed, g)
        stores[g].start()
    for store in stores:
        store.wait()


def dispatch(core, routes, tokens, dp_count):
    count, features = tokens.shape
    groups = features // GROUP
    shape = (dp_count, TILES * groups, MAIN, BLOCK)
    return pl.pallas_call(
        dispatch_kernel,
        in_specs=[SMEM, VMEM, HBM],
        out_specs=HBM,
        out_shape=jax.ShapeDtypeStruct(shape, BF16),
        scratch_shapes=[
            pltpu.VMEM(tokens.shape, BF16),
            pltpu.VMEM((dp_count * CAP, count), BF16),
            pltpu.VMEM((4 * dp_count, 4 * dp_count), BF16),
            pltpu.VMEM(shape, BF16),
            pltpu.SemaphoreType.DMA((groups,)),
            pltpu.SemaphoreType.DMA((groups,)),
        ],
        compiler_params=PARAMS,
        name="dispatch",
    )(core, routes, tokens)


def stages_of(groups):
    edges = [0, 1] + list(range(3, groups, 2)) + [groups]
    return list(zip(edges[:-1], edges[1:]))


def expert_kernel(
    core_ref,
    message_ref,
    in_own_ref,
    up_own_ref,
    in_far_ref,
    up_far_ref,
    out_own_ref,
    out_far_ref,
    back_ref,
    message,
    rows,
    in_own,
    up_own,
    in_far,
    up_far,
    out_both,
    gate_sum,
    up_sum,
    hidden,
    packed,
    pick,
    place,
    message_sem,
    weight_sem,
    far_sem,
    back_sem,
):
    core = core_ref[0]
    dp_count = message.shape[0]
    groups = message.shape[1] // TILES
    width = in_own.shape[1]
    stages = stages_of(groups)
    copy = pltpu.make_async_copy

    def stage_copies(i):
        first, last = stages[i]
        part = pl.ds(first * GROUP, (last - first) * GROUP)
        parts = pl.ds(first * TILES, (last - first) * TILES)
        return [
            copy(message_ref.at[:, parts], message.at[:, parts], message_sem.at[i]),
            copy(in_own_ref.at[core, part], in_own.at[part], weight_sem.at[2 * i]),
            copy(up_own_ref.at[core, part], up_own.at[part], weight_sem.at[2 * i + 1]),
        ]

    far_copies = [
        copy(in_far_ref, in_far, far_sem.at[0]),
        copy(up_far_ref, up_far, far_sem.at[1]),
        copy(out_own_ref.at[core], out_both.at[pl.ds(0, width)], far_sem.at[2]),
        copy(out_far_ref, out_both.at[pl.ds(width, width)], far_sem.at[3]),
    ]
    staged = [stage_copies(i) for i in range(len(stages))]
    back_copies = [copy(tiles_of(packed, g), tiles_of(back_ref, g), back_sem.at[g]) for g in range(groups)]
    for group in staged[:2]:
        for each in group:
            each.start()
    fill_pick(pick, dp_count)
    fill_place(place, dp_count)

    for i, (first, last) in enumerate(stages):
        for each in staged[i]:
            each.wait()
        if i + 2 < len(stages):
            for each in staged[i + 2]:
                each.start()
        elif i + 2 == len(stages):
            for each in far_copies[:2]:
                each.start()
        else:
            for each in far_copies[2:]:
                each.start()
        for g in range(first, last):
            rows[:, features_of(g)] = unpack(message, pick[...], g)
        part = slice(first * GROUP, last * GROUP)
        gate = dot(rows[:, part], in_own[part])
        up = dot(rows[:, part], up_own[part])
        if i > 0:
            gate = gate + gate_sum[...]
            up = up + up_sum[...]
        if i + 1 < len(stages):
            gate_sum[...] = gate
            up_sum[...] = up
        else:
            hidden[:, :width] = (gate / (1.0 + jnp.exp(-gate)) * up).astype(BF16)
    for each in far_copies[:2]:
        each.wait()
    gate = dot(rows[...], in_far[...])
    up = dot(rows[...], up_far[...])
    hidden[:, width:] = (gate / (1.0 + jnp.exp(-gate)) * up).astype(BF16)
    for each in far_copies[2:]:
        each.wait()
    for g in range(groups):
        pack(dot(hidden[...], out_both[:, features_of(g)]), place[...], packed, g)
        back_copies[g].start()
    for each in back_copies:
        each.wait()


def experts(core, message, w_in, w_up, w_out, in_far, up_far, out_far):
    dp_count, tiles = message.shape[:2]
    groups = tiles // TILES
    features, width = in_far.shape
    count = dp_count * CAP
    stages = len(stages_of(groups))
    weight = pltpu.VMEM((features, width), BF16)
    total = pltpu.VMEM((count, width), F32)
    square = pltpu.VMEM((4 * dp_count, 4 * dp_count), BF16)
    return pl.pallas_call(
        expert_kernel,
        in_specs=[SMEM] + [HBM] * 7,
        out_specs=HBM,
        out_shape=jax.ShapeDtypeStruct(message.shape, BF16),
        scratch_shapes=[
            pltpu.VMEM(message.shape, BF16),
            pltpu.VMEM((count, features), BF16),
            weight,
            weight,
            weight,
            weight,
            pltpu.VMEM((2 * width, features), BF16),
            total,
            total,
            pltpu.VMEM((count, 2 * width), BF16),
            pltpu.VMEM(message.shape, BF16),
            square,
            square,
            pltpu.SemaphoreType.DMA((stages,)),
            pltpu.SemaphoreType.DMA((2 * stages,)),
            pltpu.SemaphoreType.DMA((4,)),
            pltpu.SemaphoreType.DMA((groups,)),
        ],
        compiler_params=PARAMS,
        cost_estimate=pl.CostEstimate(
            flops=12 * count * features * width, bytes_accessed=32 * 1024 * 1024, transcendentals=0
        ),
        name="experts",
    )(core, message, w_in, w_up, in_far, up_far, w_out, out_far)


def gates_kernel(core_ref, routes_ref, gates_ref, out_ref):
    routes, gates = routes_ref[...], gates_ref[...]
    top, tokens = routes.shape
    count = out_ref.shape[1]
    dp_count = count // CAP
    code = rank_code(routes).astype(BF16)
    slots = iota((128, tokens), 0)
    value = jnp.zeros((128, tokens), F32)
    for k in range(top):
        value = value + jnp.where(routes[k : k + 1] == slots, gates[k : k + 1], 0.0)
    high = value.astype(BF16)
    low = (value - high.astype(F32)).astype(BF16)
    owner, _ = row_of(iota((128, count), 1), dp_count)
    owner = one_hot(iota((128, count), 0), 2 * owner + core_ref[0])
    _, turn = row_of(iota((tokens, count), 1), dp_count)
    here = dot(code.T, owner) == turn.astype(F32)
    for part, source in enumerate((high, low)):
        gate = jnp.where(here, dot(source.T, owner), 0.0)
        out_ref[part * tokens : (part + 1) * tokens] = gate.astype(BF16)


def spread_gates(core, routes, gates, dp_count):
    return pl.pallas_call(
        gates_kernel,
        in_specs=[SMEM, VMEM, VMEM],
        out_specs=VMEM,
        out_shape=jax.ShapeDtypeStruct((2 * routes.shape[1], dp_count * CAP), BF16),
        name="gates",
    )(core, routes, gates)


def combine_kernel(core_ref, back_ref, gates_ref, keep_ref, send_ref, message, total, pick, sem, out_sem):
    core = core_ref[0]
    dp_count = message.shape[0]
    groups = message.shape[1] // TILES
    tokens, half = keep_ref.shape
    loads = [
        pltpu.make_async_copy(tiles_of(back_ref, g), tiles_of(message, g), sem.at[g]) for g in range(groups)
    ]

    def store(side):
        part = total.at[:, pl.ds(side * half, half)]
        keep = pltpu.make_async_copy(part, keep_ref, out_sem.at[0])
        send = pltpu.make_async_copy(part, send_ref, out_sem.at[1])
        return keep, send

    for load in loads:
        load.start()
    fill_pick(pick, dp_count)
    side = 0
    for g in range(groups):
        loads[g].wait()
        value = dot(gates_ref[...], unpack(message, pick[...], g))
        total[:, features_of(g)] = value[:tokens] + value[tokens:]
        if (g + 1) * GROUP >= (side + 1) * half:
            keep, send = store(side)

            @pl.when(core == side)
            def _():
                keep.start()

            @pl.when(core != side)
            def _():
                send.start()

            side += 1
    keep, send = store(0)
    keep.wait()
    send.wait()


def combine(core, back, gates):
    dp_count, tiles = back.shape[:2]
    groups = tiles // TILES
    tokens = gates.shape[0] // 2
    out = jax.ShapeDtypeStruct((tokens, groups * GROUP // 2), F32)
    return pl.pallas_call(
        combine_kernel,
        in_specs=[SMEM, HBM, VMEM],
        out_specs=(HBM, HBM),
        out_shape=(out, out),
        scratch_shapes=[
            pltpu.VMEM(back.shape, BF16),
            pltpu.VMEM((tokens, groups * GROUP), F32),
            pltpu.VMEM((4 * dp_count, 4 * dp_count), BF16),
            pltpu.SemaphoreType.DMA((groups,)),
            pltpu.SemaphoreType.DMA((2,)),
        ],
        compiler_params=PARAMS,
        name="combine",
    )(core, back, gates)


def attention(query_latent, query_rope, cache_latent, cache_rope, lengths):
    local_span = cache_latent.shape[1]
    positions = lax.axis_index("tp") * local_span + jnp.arange(local_span, dtype=jnp.int32)
    visible = positions[None, None, :] < lengths[:, None, None]
    scores = (
        jnp.einsum("bhl,btl->bht", query_latent, cache_latent, preferred_element_type=F32)
        + jnp.einsum("bhr,brt->bht", query_rope, cache_rope, preferred_element_type=F32)
    ) * softmax_scale
    peak = jnp.max(jnp.where(visible, scores, -1e30), axis=2, keepdims=True)
    weights = jnp.where(visible, jnp.exp(scores - peak), 0.0)
    total = jnp.sum(weights, axis=2, keepdims=True)
    numer = jnp.einsum("bht,btl->bhl", weights.astype(BF16), cache_latent, preferred_element_type=F32)
    both = jnp.concatenate(
        [numer, jnp.broadcast_to(total, total.shape[:2] + (64,)), jnp.broadcast_to(peak, peak.shape[:2] + (64,))],
        axis=2,
    )
    far = lax.ppermute(both, "tp", SWAP)
    lat = numer.shape[2]
    far_numer, far_total, far_peak = far[:, :, :lat], far[:, :, lat : lat + 1], far[:, :, lat + 64 : lat + 65]
    top = jnp.maximum(peak, far_peak)
    here, there = jnp.exp(peak - top), jnp.exp(far_peak - top)
    return ((numer * here + far_numer * there) / (total * here + far_total * there)).astype(BF16)


def body(
    moe_tokens,
    slot_routes,
    route_gates,
    w_in,
    w_up,
    w_out,
    query_latent,
    query_rope,
    cache_latent,
    cache_rope,
    lengths,
):
    dp_count = lax.axis_size("dp")
    index = lax.axis_index("tp")
    core = jnp.reshape(index, (1,)).astype(jnp.int32)
    routes = slot_routes.T
    outbound = dispatch(core, routes, moe_tokens, dp_count)
    message = lax.all_to_all(outbound, "dp", split_axis=0, concat_axis=0, tiled=True)

    def swap(weight):
        return lax.ppermute(lax.dynamic_index_in_dim(weight, 1 - index, 0, False), "tp", SWAP)

    in_far, up_far, out_far = swap(w_in), swap(w_up), swap(w_out)
    gates = spread_gates(core, routes, route_gates.T, dp_count)
    back = experts(core, message, w_in, w_up, w_out, in_far, up_far, out_far)
    returned = lax.all_to_all(back, "dp", split_axis=0, concat_axis=0, tiled=True)
    keep, send = combine(core, returned, gates)
    moe_out = (keep + lax.ppermute(send, "tp", SWAP)).astype(BF16)
    attn_out = attention(query_latent, query_rope, cache_latent, cache_rope, lengths)
    return (moe_out, attn_out)


def solution(mesh):
    placed = (
        P("dp", None),
        P("dp", None),
        P("dp", None),
        P("dp", None, "tp"),
        P("dp", None, "tp"),
        P("dp", "tp", None),
        P("dp", None, None),
        P("dp", None, None),
        P("dp", "tp", None),
        P("dp", None, "tp"),
        P("dp"),
    )
    return jax.shard_map(
        body,
        mesh=mesh,
        in_specs=placed,
        out_specs=(P("dp", "tp"), P("dp", None, None)),
        check_vma=False,
    )
```

```python
import math

import jax
import jax.numpy as jnp
from jax import lax
from jax.experimental import pallas as pl
from jax.experimental.pallas import tpu as pltpu
from jax.sharding import PartitionSpec as P

softmax_scale = 192.0 ** (-0.5) * (0.1 * math.log(40.0) + 1.0) ** 2

GROUP = 512
BLOCK = 128
TILES = 5
MAIN = 8
REST = 2
CAP = 10
F32 = jnp.float32
BF16 = jnp.bfloat16
SWAP = ((0, 1), (1, 0))
HBM = pl.BlockSpec(memory_space=pl.ANY)
VMEM = pl.BlockSpec(memory_space=pltpu.VMEM)
SMEM = pl.BlockSpec(memory_space=pltpu.SMEM)
PARAMS = pltpu.CompilerParams(vmem_limit_bytes=58 * 1024 * 1024)


def dot(a, b):
    return jnp.dot(a, b, preferred_element_type=F32)


def iota(shape, dim):
    return lax.broadcasted_iota(jnp.int32, shape, dim)


def one_hot(a, b):
    return (a == b).astype(F32).astype(BF16)


def tiles_of(ref, group):
    return ref.at[:, pl.ds(group * TILES, TILES)]


def pack_copies(packed, messages, sems, groups):
    copies = []
    for g in range(groups):
        for i, part in enumerate((pl.ds(g * TILES, TILES - 1), pl.ds(g * TILES + TILES - 1, 1))):
            copies.append(pltpu.make_async_copy(packed.at[:, part], messages.at[:, part], sems.at[2 * g + i]))
    return copies


def start(copies):
    for each in copies:
        each.start()


def wait(copies):
    for each in copies:
        each.wait()


def features_of(group):
    return slice(group * GROUP, (group + 1) * GROUP)


def block_of(f):
    return slice(f * BLOCK, (f + 1) * BLOCK)


def unit_of(row, half):
    return ((row & (2 * half - 1)) >> 1) * MAIN + lax.div(row, 2 * half) * REST + (row & 1)


def fill_place(ref, dp_count):
    size = ref.shape[0]
    ref[...] = one_hot(iota((size, size), 0), unit_of(iota((size, size), 1), dp_count // 2))


def fill_pick(ref, dp_count):
    size = ref.shape[0]
    ref[...] = one_hot(iota((size, size), 1), unit_of(iota((size, size), 0), dp_count // 2))


def pack(value, ref, group):
    dp_count = ref.shape[0]
    main, half = dp_count * MAIN, dp_count // 2
    for f in range(4):
        part = value[:main, block_of(f)].astype(BF16)
        ref[:, group * TILES + f] = part.reshape(dp_count, MAIN, BLOCK)
    rest = value[main:].astype(BF16)
    sides = [rest[: 2 * half], rest[2 * half :]]
    sides = [jnp.concatenate([side[:, block_of(f)] for f in range(4)], axis=0) for side in sides]
    return jnp.concatenate(sides, axis=1)


def place_rest(rest, place, ref, group):
    half = ref.shape[0] // 2
    rest = dot(place, rest)
    for h in range(2):
        part = rest[:, block_of(h)].astype(BF16)
        ref[h * half : (h + 1) * half, group * TILES + 4] = part.reshape(half, MAIN, BLOCK)


def pack_all(groups, value_of, place, packed, copies):
    rest = None
    for g in range(groups):
        value = value_of(g)
        if rest is not None:
            place_rest(rest, place, packed, g - 1)
        rest = pack(value, packed, g)
        start([copies[2 * g]] + ([copies[2 * g - 1]] if g else []))
    place_rest(rest, place, packed, groups - 1)
    start(copies[-1:])
    wait(copies)


def pick_rest(ref, pick, group):
    dp_count = ref.shape[0]
    main, half = dp_count * MAIN, dp_count // 2
    rest = ref[:, group * TILES + 4].reshape(main, BLOCK)
    rest = dot(pick, jnp.concatenate([rest[: main // 2], rest[main // 2 :]], axis=1)).astype(BF16)
    sides = [
        jnp.concatenate([rest[2 * half * f : 2 * half * (f + 1), block_of(h)] for f in range(4)], axis=1)
        for h in range(2)
    ]
    return jnp.concatenate(sides, axis=0)


def main_rows(ref, group):
    main = ref.shape[0] * MAIN
    return jnp.concatenate([ref[:, group * TILES + f].reshape(main, BLOCK) for f in range(4)], axis=1)


def row_of(index, dp_count):
    main = dp_count * MAIN
    first = index < main
    after = index - main
    return jnp.where(first, index >> 3, after >> 1), jnp.where(first, index & 7, MAIN + (after & 1))


def rank_code(routes):
    top, tokens = routes.shape
    slots = iota((128, tokens), 0)
    named = jnp.zeros((128, tokens), F32)
    for k in range(top):
        named = named + (routes[k : k + 1] == slots).astype(F32)
    earlier = (iota((tokens, tokens), 0) < iota((tokens, tokens), 1)).astype(F32).astype(BF16)
    rank = dot(named.astype(BF16), earlier)
    return jnp.where(named > 0.0, rank, -1.0)


def dispatch_kernel(core_ref, routes_ref, tokens_ref, out_ref, rows, chosen, place, packed, in_sem, out_sem):
    dp_count = out_ref.shape[0]
    groups = out_ref.shape[1] // TILES
    loads = [
        pltpu.make_async_copy(tokens_ref.at[:, features_of(g)], rows.at[:, features_of(g)], in_sem.at[g])
        for g in range(groups)
    ]
    start(loads)
    fill_place(place, dp_count)
    code = rank_code(routes_ref[...]).astype(BF16)
    tokens = code.shape[1]
    count = dp_count * CAP
    owner, _ = row_of(iota((count, 128), 0), dp_count)
    spread = dot(one_hot(iota((count, 128), 1), 2 * owner + core_ref[0]), code)
    _, turn = row_of(iota((count, tokens), 0), dp_count)
    chosen[...] = one_hot(spread, turn.astype(F32))
    wait(loads)
    stores = pack_copies(packed, out_ref, out_sem, groups)
    pack_all(groups, lambda g: dot(chosen[...], rows[:, features_of(g)]), place[...], packed, stores)


def dispatch(core, routes, tokens, dp_count):
    count, features = tokens.shape
    groups = features // GROUP
    shape = (dp_count, TILES * groups, MAIN, BLOCK)
    return pl.pallas_call(
        dispatch_kernel,
        in_specs=[SMEM, VMEM, HBM],
        out_specs=HBM,
        out_shape=jax.ShapeDtypeStruct(shape, BF16),
        scratch_shapes=[
            pltpu.VMEM(tokens.shape, BF16),
            pltpu.VMEM((dp_count * CAP, count), BF16),
            pltpu.VMEM((4 * dp_count, 4 * dp_count), BF16),
            pltpu.VMEM(shape, BF16),
            pltpu.SemaphoreType.DMA((groups,)),
            pltpu.SemaphoreType.DMA((2 * groups,)),
        ],
        compiler_params=PARAMS,
        name="dispatch",
    )(core, routes, tokens)


def stages_of(groups):
    edges = [0, 1] + list(range(3, groups, 2)) + [groups]
    return list(zip(edges[:-1], edges[1:]))


def expert_kernel(
    core_ref,
    message_ref,
    in_own_ref,
    up_own_ref,
    in_far_ref,
    up_far_ref,
    out_own_ref,
    out_far_ref,
    back_ref,
    message,
    rows,
    in_own,
    up_own,
    in_far,
    up_far,
    out_both,
    gate_sum,
    up_sum,
    hidden,
    packed,
    pick,
    place,
    message_sem,
    weight_sem,
    far_sem,
    back_sem,
):
    core = core_ref[0]
    dp_count = message.shape[0]
    groups = message.shape[1] // TILES
    width = in_own.shape[1]
    stages = stages_of(groups)
    copy = pltpu.make_async_copy

    def stage_copies(i):
        first, last = stages[i]
        part = pl.ds(first * GROUP, (last - first) * GROUP)
        return [
            copy(in_own_ref.at[core, part], in_own.at[part], weight_sem.at[2 * i]),
            copy(up_own_ref.at[core, part], up_own.at[part], weight_sem.at[2 * i + 1]),
        ]

    def message_copy(i):
        first, last = stages[i]
        part = pl.ds(first * TILES, (last - first) * TILES)
        return copy(message_ref.at[:, part], message.at[:, part], message_sem.at[i])

    def unpack(i):
        for g in range(*stages[i]):
            rows[: dp_count * MAIN, features_of(g)] = main_rows(message, g)
            rows[dp_count * MAIN :, features_of(g)] = pick_rest(message, pick[...], g)

    far_copies = [
        copy(in_far_ref, in_far, far_sem.at[0]),
        copy(up_far_ref, up_far, far_sem.at[1]),
        copy(out_own_ref.at[core], out_both.at[pl.ds(0, width)], far_sem.at[2]),
        copy(out_far_ref, out_both.at[pl.ds(width, width)], far_sem.at[3]),
    ]
    staged = [stage_copies(i) for i in range(len(stages))] + [far_copies[:2], far_copies[2:]]
    messages = [message_copy(i) for i in range(len(stages))]
    back_copies = pack_copies(packed, back_ref, back_sem, groups)
    start([messages[0]] + staged[0] + [messages[1]] + staged[1] + [messages[2]] + staged[2])
    fill_pick(pick, dp_count)
    fill_place(place, dp_count)
    wait(messages[:1])
    unpack(0)

    for i, (first, last) in enumerate(stages):
        wait(staged[i])
        if i + 3 < len(staged):
            start(messages[i + 3 : i + 4] + staged[i + 3])
        if 0 < i < len(stages) - 1:
            wait([messages[i + 1]])
            unpack(i + 1)
        part = slice(first * GROUP, last * GROUP)
        gate = dot(rows[:, part], in_own[part])
        up = dot(rows[:, part], up_own[part])
        if i > 0:
            gate = gate + gate_sum[...]
            up = up + up_sum[...]
        if i + 1 < len(stages):
            gate_sum[...] = gate
            up_sum[...] = up
        else:
            hidden[:, :width] = (gate / (1.0 + jnp.exp(-gate)) * up).astype(BF16)
        if i == 0:
            wait([messages[1]])
            unpack(1)
    wait(far_copies[:2])
    gate = dot(rows[...], in_far[...])
    up = dot(rows[...], up_far[...])
    hidden[:, width:] = (gate / (1.0 + jnp.exp(-gate)) * up).astype(BF16)
    wait(far_copies[2:])
    pack_all(groups, lambda g: dot(hidden[...], out_both[:, features_of(g)]), place[...], packed, back_copies)


def experts(core, message, w_in, w_up, w_out, in_far, up_far, out_far):
    dp_count, tiles = message.shape[:2]
    groups = tiles // TILES
    features, width = in_far.shape
    count = dp_count * CAP
    stages = len(stages_of(groups))
    weight = pltpu.VMEM((features, width), BF16)
    total = pltpu.VMEM((count, width), F32)
    square = pltpu.VMEM((4 * dp_count, 4 * dp_count), BF16)
    return pl.pallas_call(
        expert_kernel,
        in_specs=[SMEM] + [HBM] * 7,
        out_specs=HBM,
        out_shape=jax.ShapeDtypeStruct(message.shape, BF16),
        scratch_shapes=[
            pltpu.VMEM(message.shape, BF16),
            pltpu.VMEM((count, features), BF16),
            weight,
            weight,
            weight,
            weight,
            pltpu.VMEM((2 * width, features), BF16),
            total,
            total,
            pltpu.VMEM((count, 2 * width), BF16),
            pltpu.VMEM(message.shape, BF16),
            square,
            square,
            pltpu.SemaphoreType.DMA((stages,)),
            pltpu.SemaphoreType.DMA((2 * stages,)),
            pltpu.SemaphoreType.DMA((4,)),
            pltpu.SemaphoreType.DMA((2 * groups,)),
        ],
        compiler_params=PARAMS,
        cost_estimate=pl.CostEstimate(
            flops=12 * count * features * width, bytes_accessed=32 * 1024 * 1024, transcendentals=0
        ),
        name="experts",
    )(core, message, w_in, w_up, in_far, up_far, w_out, out_far)


def gates_kernel(core_ref, routes_ref, gates_ref, out_ref):
    routes, gates = routes_ref[...], gates_ref[...]
    top, tokens = routes.shape
    count = out_ref.shape[1]
    dp_count = count // CAP
    code = rank_code(routes).astype(BF16)
    slots = iota((128, tokens), 0)
    value = jnp.zeros((128, tokens), F32)
    for k in range(top):
        value = value + jnp.where(routes[k : k + 1] == slots, gates[k : k + 1], 0.0)
    high = value.astype(BF16)
    low = (value - high.astype(F32)).astype(BF16)
    owner, _ = row_of(iota((128, count), 1), dp_count)
    owner = one_hot(iota((128, count), 0), 2 * owner + core_ref[0])
    _, turn = row_of(iota((tokens, count), 1), dp_count)
    here = dot(code.T, owner) == turn.astype(F32)
    for part, source in enumerate((high, low)):
        gate = jnp.where(here, dot(source.T, owner), 0.0)
        out_ref[part * tokens : (part + 1) * tokens] = gate.astype(BF16)


def spread_gates(core, routes, gates, dp_count):
    return pl.pallas_call(
        gates_kernel,
        in_specs=[SMEM, VMEM, VMEM],
        out_specs=VMEM,
        out_shape=jax.ShapeDtypeStruct((2 * routes.shape[1], dp_count * CAP), BF16),
        name="gates",
    )(core, routes, gates)


def combine_kernel(core_ref, back_ref, gates_ref, after_ref, keep_ref, send_ref, message, gates, total, pick, sem):
    core = core_ref[0]
    dp_count = message.shape[0]
    groups = message.shape[1] // TILES
    tokens, half = keep_ref.shape
    loads = [
        pltpu.make_async_copy(tiles_of(back_ref, g), tiles_of(message, g), sem.at[g]) for g in range(groups)
    ]
    gates_load = [pltpu.make_async_copy(gates_ref, gates, sem.at[groups])]
    start(gates_load + loads)
    fill_pick(pick, dp_count)
    wait(gates_load + loads[:1])
    rest = pick_rest(message, pick[...], 0)
    side = 0
    for g in range(groups):
        wait(loads[g + 1 : g + 2])
        value = dot(gates[...], jnp.concatenate([main_rows(message, g), rest], axis=0))
        if g + 1 < groups:
            rest = pick_rest(message, pick[...], g + 1)
        total[:, features_of(g)] = value[:tokens] + value[tokens:]
        if (g + 1) * GROUP >= (side + 1) * half:
            part = slice(side * half, (side + 1) * half)

            @pl.when(core == side)
            def _():
                keep_ref[...] = total[:, part]

            @pl.when(core != side)
            def _():
                send_ref[...] = total[:, part]

            side += 1


def combine(core, back, gates, after):
    dp_count, tiles = back.shape[:2]
    groups = tiles // TILES
    tokens = gates.shape[0] // 2
    out = jax.ShapeDtypeStruct((tokens, groups * GROUP // 2), F32)
    return pl.pallas_call(
        combine_kernel,
        in_specs=[SMEM, HBM, HBM, HBM],
        out_specs=(VMEM, VMEM),
        out_shape=(out, out),
        scratch_shapes=[
            pltpu.VMEM(back.shape, BF16),
            pltpu.VMEM(gates.shape, BF16),
            pltpu.VMEM((tokens, groups * GROUP), F32),
            pltpu.VMEM((4 * dp_count, 4 * dp_count), BF16),
            pltpu.SemaphoreType.DMA((groups + 1,)),
        ],
        compiler_params=pltpu.CompilerParams(vmem_limit_bytes=16 * 1024 * 1024),
        name="combine",
    )(core, back, gates, after)


def attention(query_latent, query_rope, cache_latent, cache_rope, lengths):
    local_span = cache_latent.shape[1]
    positions = lax.axis_index("tp") * local_span + jnp.arange(local_span, dtype=jnp.int32)
    visible = positions[None, None, :] < lengths[:, None, None]
    scores = (
        jnp.einsum("bhl,btl->bht", query_latent, cache_latent, preferred_element_type=F32)
        + jnp.einsum("bhr,brt->bht", query_rope, cache_rope, preferred_element_type=F32)
    ) * softmax_scale
    peak = jnp.max(jnp.where(visible, scores, -1e30), axis=2, keepdims=True)
    weights = jnp.where(visible, jnp.exp(scores - peak), 0.0)
    total = jnp.sum(weights, axis=2, keepdims=True)
    numer = jnp.einsum("bht,btl->bhl", weights.astype(BF16), cache_latent, preferred_element_type=F32)
    both = jnp.concatenate(
        [numer, jnp.broadcast_to(total, total.shape[:2] + (64,)), jnp.broadcast_to(peak, peak.shape[:2] + (64,))],
        axis=2,
    )
    far = lax.ppermute(both, "tp", SWAP)
    lat = numer.shape[2]
    far_numer, far_total, far_peak = far[:, :, :lat], far[:, :, lat : lat + 1], far[:, :, lat + 64 : lat + 65]
    top = jnp.maximum(peak, far_peak)
    here, there = jnp.exp(peak - top), jnp.exp(far_peak - top)
    return ((numer * here + far_numer * there) / (total * here + far_total * there)).astype(BF16)


def body(
    moe_tokens,
    slot_routes,
    route_gates,
    w_in,
    w_up,
    w_out,
    query_latent,
    query_rope,
    cache_latent,
    cache_rope,
    lengths,
):
    dp_count = lax.axis_size("dp")
    index = lax.axis_index("tp")
    core = jnp.reshape(index, (1,)).astype(jnp.int32)
    routes = slot_routes.T
    outbound = dispatch(core, routes, moe_tokens, dp_count)
    message = lax.all_to_all(outbound, "dp", split_axis=0, concat_axis=0, tiled=True)

    def swap(weight):
        return lax.ppermute(lax.dynamic_index_in_dim(weight, 1 - index, 0, False), "tp", SWAP)

    in_far, up_far, out_far = swap(w_in), swap(w_up), swap(w_out)
    gates = spread_gates(core, routes, route_gates.T, dp_count)
    back = experts(core, message, w_in, w_up, w_out, in_far, up_far, out_far)
    returned = lax.all_to_all(back, "dp", split_axis=0, concat_axis=0, tiled=True)
    attn_out = attention(query_latent, query_rope, cache_latent, cache_rope, lengths)
    keep, send = combine(core, returned, gates, attn_out)
    moe_out = (keep + lax.ppermute(send, "tp", SWAP)).astype(BF16)
    return (moe_out, attn_out)


def solution(mesh):
    placed = (
        P("dp", None),
        P("dp", None),
        P("dp", None),
        P("dp", None, "tp"),
        P("dp", None, "tp"),
        P("dp", "tp", None),
        P("dp", None, None),
        P("dp", None, None),
        P("dp", "tp", None),
        P("dp", None, "tp"),
        P("dp"),
    )
    return jax.shard_map(
        body,
        mesh=mesh,
        in_specs=placed,
        out_specs=(P("dp", "tp"), P("dp", None, None)),
        check_vma=False,
    )
```

```python
import math

import jax
import jax.numpy as jnp
from jax import lax
from jax.experimental import pallas as pl
from jax.experimental.pallas import tpu as pltpu
from jax.sharding import PartitionSpec as P

softmax_scale = 192.0 ** (-0.5) * (0.1 * math.log(40.0) + 1.0) ** 2

GROUP = 512
BLOCK = 128
TILES = 5
MAIN = 8
REST = 2
CAP = 10
F32 = jnp.float32
BF16 = jnp.bfloat16
SWAP = ((0, 1), (1, 0))
HBM = pl.BlockSpec(memory_space=pl.ANY)
VMEM = pl.BlockSpec(memory_space=pltpu.VMEM)
SMEM = pl.BlockSpec(memory_space=pltpu.SMEM)
PARAMS = pltpu.CompilerParams(vmem_limit_bytes=58 * 1024 * 1024)


def dot(a, b):
    return jnp.dot(a, b, preferred_element_type=F32)


def iota(shape, dim):
    return lax.broadcasted_iota(jnp.int32, shape, dim)


def one_hot(a, b):
    return (a == b).astype(F32).astype(BF16)


def tiles_of(ref, group):
    return ref.at[:, pl.ds(group * TILES, TILES)]


def pack_copies(packed, messages, sems, groups):
    copies = []
    for g in range(groups):
        for i, part in enumerate((pl.ds(g * TILES, TILES - 1), pl.ds(g * TILES + TILES - 1, 1))):
            copies.append(pltpu.make_async_copy(packed.at[:, part], messages.at[:, part], sems.at[2 * g + i]))
    return copies


def start(copies):
    for each in copies:
        each.start()


def wait(copies):
    for each in copies:
        each.wait()


def features_of(group):
    return slice(group * GROUP, (group + 1) * GROUP)


def block_of(f):
    return slice(f * BLOCK, (f + 1) * BLOCK)


def unit_of(row, half):
    return ((row & (2 * half - 1)) >> 1) * MAIN + lax.div(row, 2 * half) * REST + (row & 1)


def fill_place(ref, dp_count):
    size = ref.shape[0]
    ref[...] = one_hot(iota((size, size), 0), unit_of(iota((size, size), 1), dp_count // 2))


def fill_pick(ref, dp_count):
    size = ref.shape[0]
    ref[...] = one_hot(iota((size, size), 1), unit_of(iota((size, size), 0), dp_count // 2))


def pack(value, ref, group):
    dp_count = ref.shape[0]
    main, half = dp_count * MAIN, dp_count // 2
    for f in range(4):
        part = value[:main, block_of(f)].astype(BF16)
        ref[:, group * TILES + f] = part.reshape(dp_count, MAIN, BLOCK)
    rest = value[main:].astype(BF16)
    sides = [rest[: 2 * half], rest[2 * half :]]
    sides = [jnp.concatenate([side[:, block_of(f)] for f in range(4)], axis=0) for side in sides]
    return jnp.concatenate(sides, axis=1)


def place_rest(rest, place, ref, group):
    half = ref.shape[0] // 2
    rest = dot(place, rest)
    for h in range(2):
        part = rest[:, block_of(h)].astype(BF16)
        ref[h * half : (h + 1) * half, group * TILES + 4] = part.reshape(half, MAIN, BLOCK)


def pack_all(groups, value_of, place, packed, copies):
    rest = None
    for g in range(groups):
        value = value_of(g)
        if rest is not None:
            place_rest(rest, place, packed, g - 1)
        rest = pack(value, packed, g)
        start([copies[2 * g]] + ([copies[2 * g - 1]] if g else []))
    place_rest(rest, place, packed, groups - 1)
    start(copies[-1:])
    wait(copies)


def pick_rest(ref, pick, group):
    dp_count = ref.shape[0]
    main, half = dp_count * MAIN, dp_count // 2
    rest = ref[:, group * TILES + 4].reshape(main, BLOCK)
    rest = dot(pick, jnp.concatenate([rest[: main // 2], rest[main // 2 :]], axis=1)).astype(BF16)
    sides = [
        jnp.concatenate([rest[2 * half * f : 2 * half * (f + 1), block_of(h)] for f in range(4)], axis=1)
        for h in range(2)
    ]
    return jnp.concatenate(sides, axis=0)


def main_rows(ref, group):
    main = ref.shape[0] * MAIN
    return jnp.concatenate([ref[:, group * TILES + f].reshape(main, BLOCK) for f in range(4)], axis=1)


def row_of(index, dp_count):
    main = dp_count * MAIN
    first = index < main
    after = index - main
    return jnp.where(first, index >> 3, after >> 1), jnp.where(first, index & 7, MAIN + (after & 1))


def rank_code(routes):
    top, tokens = routes.shape
    slots = iota((128, tokens), 0)
    named = jnp.zeros((128, tokens), F32)
    for k in range(top):
        named = named + (routes[k : k + 1] == slots).astype(F32)
    earlier = (iota((tokens, tokens), 0) < iota((tokens, tokens), 1)).astype(F32).astype(BF16)
    rank = dot(named.astype(BF16), earlier)
    return jnp.where(named > 0.0, rank, -1.0)


def dispatch_kernel(
    core_ref, routes_ref, tokens_ref, out_ref, routes, rows, chosen, place, packed, in_sem, out_sem
):
    dp_count = out_ref.shape[0]
    groups = out_ref.shape[1] // TILES
    loads = [
        pltpu.make_async_copy(tokens_ref.at[:, features_of(g)], rows.at[:, features_of(g)], in_sem.at[g])
        for g in range(groups)
    ]
    routes_load = pltpu.make_async_copy(routes_ref, routes, in_sem.at[groups])
    start([routes_load] + loads)
    fill_place(place, dp_count)
    wait([routes_load])
    code = rank_code(routes[...]).astype(BF16)
    tokens = code.shape[1]
    count = dp_count * CAP
    owner, _ = row_of(iota((count, 128), 0), dp_count)
    spread = dot(one_hot(iota((count, 128), 1), 2 * owner + core_ref[0]), code)
    _, turn = row_of(iota((count, tokens), 0), dp_count)
    chosen[...] = one_hot(spread, turn.astype(F32))
    wait(loads)
    stores = pack_copies(packed, out_ref, out_sem, groups)
    pack_all(groups, lambda g: dot(chosen[...], rows[:, features_of(g)]), place[...], packed, stores)


def dispatch(core, routes, tokens, dp_count):
    count, features = tokens.shape
    groups = features // GROUP
    shape = (dp_count, TILES * groups, MAIN, BLOCK)
    return pl.pallas_call(
        dispatch_kernel,
        in_specs=[SMEM, HBM, HBM],
        out_specs=HBM,
        out_shape=jax.ShapeDtypeStruct(shape, BF16),
        scratch_shapes=[
            pltpu.VMEM(routes.shape, jnp.int32),
            pltpu.VMEM(tokens.shape, BF16),
            pltpu.VMEM((dp_count * CAP, count), BF16),
            pltpu.VMEM((4 * dp_count, 4 * dp_count), BF16),
            pltpu.VMEM(shape, BF16),
            pltpu.SemaphoreType.DMA((groups + 1,)),
            pltpu.SemaphoreType.DMA((2 * groups,)),
        ],
        compiler_params=PARAMS,
        name="dispatch",
    )(core, routes, tokens)


def stages_of(groups):
    edges = [0, 1] + list(range(3, groups, 2)) + [groups]
    return list(zip(edges[:-1], edges[1:]))


def expert_kernel(
    core_ref,
    message_ref,
    in_own_ref,
    up_own_ref,
    in_far_ref,
    up_far_ref,
    out_own_ref,
    out_far_ref,
    back_ref,
    message,
    rows,
    in_own,
    up_own,
    in_far,
    up_far,
    out_both,
    gate_sum,
    up_sum,
    hidden,
    packed,
    pick,
    place,
    message_sem,
    weight_sem,
    far_sem,
    back_sem,
):
    core = core_ref[0]
    dp_count = message.shape[0]
    groups = message.shape[1] // TILES
    width = in_own.shape[1]
    stages = stages_of(groups)
    copy = pltpu.make_async_copy

    def stage_copies(i):
        first, last = stages[i]
        part = pl.ds(first * GROUP, (last - first) * GROUP)
        return [
            copy(in_own_ref.at[core, part], in_own.at[part], weight_sem.at[2 * i]),
            copy(up_own_ref.at[core, part], up_own.at[part], weight_sem.at[2 * i + 1]),
        ]

    def message_copy(i):
        first, last = stages[i]
        part = pl.ds(first * TILES, (last - first) * TILES)
        return copy(message_ref.at[:, part], message.at[:, part], message_sem.at[i])

    def unpack(i):
        for g in range(*stages[i]):
            rows[: dp_count * MAIN, features_of(g)] = main_rows(message, g)
            rows[dp_count * MAIN :, features_of(g)] = pick_rest(message, pick[...], g)

    far_copies = [
        copy(in_far_ref, in_far, far_sem.at[0]),
        copy(up_far_ref, up_far, far_sem.at[1]),
        copy(out_own_ref.at[core], out_both.at[pl.ds(0, width)], far_sem.at[2]),
        copy(out_far_ref, out_both.at[pl.ds(width, width)], far_sem.at[3]),
    ]
    staged = [stage_copies(i) for i in range(len(stages))] + [far_copies[:2], far_copies[2:]]
    messages = [message_copy(i) for i in range(len(stages))]
    back_copies = pack_copies(packed, back_ref, back_sem, groups)
    start(messages + staged[0] + staged[1] + staged[2])
    fill_pick(pick, dp_count)
    fill_place(place, dp_count)
    wait(messages[:1])
    unpack(0)

    for i, (first, last) in enumerate(stages):
        wait(staged[i])
        if i + 3 < len(staged):
            start(staged[i + 3])
        if 0 < i < len(stages) - 1:
            wait([messages[i + 1]])
            unpack(i + 1)
        part = slice(first * GROUP, last * GROUP)
        gate = dot(rows[:, part], in_own[part])
        up = dot(rows[:, part], up_own[part])
        if i > 0:
            gate = gate + gate_sum[...]
            up = up + up_sum[...]
        if i + 1 < len(stages):
            gate_sum[...] = gate
            up_sum[...] = up
        else:
            hidden[:, :width] = (gate / (1.0 + jnp.exp(-gate)) * up).astype(BF16)
        if i == 0:
            wait([messages[1]])
            unpack(1)
    wait(far_copies[:2])
    gate = dot(rows[...], in_far[...])
    up = dot(rows[...], up_far[...])
    hidden[:, width:] = (gate / (1.0 + jnp.exp(-gate)) * up).astype(BF16)
    wait(far_copies[2:])
    pack_all(groups, lambda g: dot(hidden[...], out_both[:, features_of(g)]), place[...], packed, back_copies)


def experts(core, message, w_in, w_up, w_out, in_far, up_far, out_far):
    dp_count, tiles = message.shape[:2]
    groups = tiles // TILES
    features, width = in_far.shape
    count = dp_count * CAP
    stages = len(stages_of(groups))
    weight = pltpu.VMEM((features, width), BF16)
    total = pltpu.VMEM((count, width), F32)
    square = pltpu.VMEM((4 * dp_count, 4 * dp_count), BF16)
    return pl.pallas_call(
        expert_kernel,
        in_specs=[SMEM] + [HBM] * 7,
        out_specs=HBM,
        out_shape=jax.ShapeDtypeStruct(message.shape, BF16),
        scratch_shapes=[
            pltpu.VMEM(message.shape, BF16),
            pltpu.VMEM((count, features), BF16),
            weight,
            weight,
            weight,
            weight,
            pltpu.VMEM((2 * width, features), BF16),
            total,
            total,
            pltpu.VMEM((count, 2 * width), BF16),
            pltpu.VMEM(message.shape, BF16),
            square,
            square,
            pltpu.SemaphoreType.DMA((stages,)),
            pltpu.SemaphoreType.DMA((2 * stages,)),
            pltpu.SemaphoreType.DMA((4,)),
            pltpu.SemaphoreType.DMA((2 * groups,)),
        ],
        compiler_params=PARAMS,
        cost_estimate=pl.CostEstimate(
            flops=12 * count * features * width, bytes_accessed=32 * 1024 * 1024, transcendentals=0
        ),
        name="experts",
    )(core, message, w_in, w_up, in_far, up_far, w_out, out_far)


def spread_gates(core, routes, gates, out_ref):
    top, tokens = routes.shape
    count = out_ref.shape[1]
    dp_count = count // CAP
    code = rank_code(routes).astype(BF16)
    slots = iota((128, tokens), 0)
    value = jnp.zeros((128, tokens), F32)
    for k in range(top):
        value = value + jnp.where(routes[k : k + 1] == slots, gates[k : k + 1], 0.0)
    high = value.astype(BF16)
    low = (value - high.astype(F32)).astype(BF16)
    owner, _ = row_of(iota((128, count), 1), dp_count)
    owner = one_hot(iota((128, count), 0), 2 * owner + core)
    _, turn = row_of(iota((tokens, count), 1), dp_count)
    here = dot(code.T, owner) == turn.astype(F32)
    for part, source in enumerate((high, low)):
        gate = jnp.where(here, dot(source.T, owner), 0.0)
        out_ref[part * tokens : (part + 1) * tokens] = gate.astype(BF16)


def combine_kernel(
    core_ref,
    back_ref,
    routes_ref,
    gates_ref,
    after_ref,
    keep_ref,
    send_ref,
    message,
    routes,
    gates,
    spread,
    total,
    pick,
    sem,
):
    core = core_ref[0]
    dp_count = message.shape[0]
    groups = message.shape[1] // TILES
    tokens, half = keep_ref.shape
    loads = [
        pltpu.make_async_copy(tiles_of(back_ref, g), tiles_of(message, g), sem.at[g]) for g in range(groups)
    ]
    first = [
        pltpu.make_async_copy(routes_ref, routes, sem.at[groups]),
        pltpu.make_async_copy(gates_ref, gates, sem.at[groups + 1]),
    ]
    start(first + loads)
    fill_pick(pick, dp_count)
    wait(first)
    spread_gates(core, routes[...], gates[...], spread)
    wait(loads[:1])
    rest = pick_rest(message, pick[...], 0)
    side = 0
    for g in range(groups):
        wait(loads[g + 1 : g + 2])
        value = dot(spread[...], jnp.concatenate([main_rows(message, g), rest], axis=0))
        if g + 1 < groups:
            rest = pick_rest(message, pick[...], g + 1)
        total[:, features_of(g)] = value[:tokens] + value[tokens:]
        if (g + 1) * GROUP >= (side + 1) * half:
            part = slice(side * half, (side + 1) * half)

            @pl.when(core == side)
            def _():
                keep_ref[...] = total[:, part]

            @pl.when(core != side)
            def _():
                send_ref[...] = total[:, part]

            side += 1


def combine(core, back, routes, gates, after):
    dp_count, tiles = back.shape[:2]
    groups = tiles // TILES
    tokens = routes.shape[1]
    out = jax.ShapeDtypeStruct((tokens, groups * GROUP // 2), F32)
    return pl.pallas_call(
        combine_kernel,
        in_specs=[SMEM, HBM, HBM, HBM, HBM],
        out_specs=(VMEM, VMEM),
        out_shape=(out, out),
        scratch_shapes=[
            pltpu.VMEM(back.shape, BF16),
            pltpu.VMEM(routes.shape, jnp.int32),
            pltpu.VMEM(gates.shape, F32),
            pltpu.VMEM((2 * tokens, dp_count * CAP), BF16),
            pltpu.VMEM((tokens, groups * GROUP), F32),
            pltpu.VMEM((4 * dp_count, 4 * dp_count), BF16),
            pltpu.SemaphoreType.DMA((groups + 2,)),
        ],
        compiler_params=pltpu.CompilerParams(vmem_limit_bytes=16 * 1024 * 1024),
        name="combine",
    )(core, back, routes, gates, after)


def attention(query_latent, query_rope, cache_latent, cache_rope, lengths):
    local_span = cache_latent.shape[1]
    positions = lax.axis_index("tp") * local_span + jnp.arange(local_span, dtype=jnp.int32)
    visible = positions[None, None, :] < lengths[:, None, None]
    scores = (
        jnp.einsum("bhl,btl->bht", query_latent, cache_latent, preferred_element_type=F32)
        + jnp.einsum("bhr,brt->bht", query_rope, cache_rope, preferred_element_type=F32)
    ) * softmax_scale
    peak = jnp.max(jnp.where(visible, scores, -1e30), axis=2, keepdims=True)
    weights = jnp.where(visible, jnp.exp(scores - peak), 0.0)
    total = jnp.sum(weights, axis=2, keepdims=True)
    numer = jnp.einsum("bht,btl->bhl", weights.astype(BF16), cache_latent, preferred_element_type=F32)
    both = jnp.concatenate(
        [numer, jnp.broadcast_to(total, total.shape[:2] + (64,)), jnp.broadcast_to(peak, peak.shape[:2] + (64,))],
        axis=2,
    )
    far = lax.ppermute(both, "tp", SWAP)
    lat = numer.shape[2]
    far_numer, far_total, far_peak = far[:, :, :lat], far[:, :, lat : lat + 1], far[:, :, lat + 64 : lat + 65]
    top = jnp.maximum(peak, far_peak)
    here, there = jnp.exp(peak - top), jnp.exp(far_peak - top)
    return ((numer * here + far_numer * there) / (total * here + far_total * there)).astype(BF16)


def body(
    moe_tokens,
    slot_routes,
    route_gates,
    w_in,
    w_up,
    w_out,
    query_latent,
    query_rope,
    cache_latent,
    cache_rope,
    lengths,
):
    dp_count = lax.axis_size("dp")
    index = lax.axis_index("tp")
    core = jnp.reshape(index, (1,)).astype(jnp.int32)
    routes = slot_routes.T
    outbound = dispatch(core, routes, moe_tokens, dp_count)
    message = lax.all_to_all(outbound, "dp", split_axis=0, concat_axis=0, tiled=True)

    def swap(weight):
        return lax.ppermute(lax.dynamic_index_in_dim(weight, 1 - index, 0, False), "tp", SWAP)

    in_far, up_far, out_far = swap(w_in), swap(w_up), swap(w_out)
    back = experts(core, message, w_in, w_up, w_out, in_far, up_far, out_far)
    returned = lax.all_to_all(back, "dp", split_axis=0, concat_axis=0, tiled=True)
    attn_out = attention(query_latent, query_rope, cache_latent, cache_rope, lengths)
    keep, send = combine(core, returned, routes, route_gates.T, attn_out)
    moe_out = (keep + lax.ppermute(send, "tp", SWAP)).astype(BF16)
    return (moe_out, attn_out)


def solution(mesh):
    placed = (
        P("dp", None),
        P("dp", None),
        P("dp", None),
        P("dp", None, "tp"),
        P("dp", None, "tp"),
        P("dp", "tp", None),
        P("dp", None, None),
        P("dp", None, None),
        P("dp", "tp", None),
        P("dp", None, "tp"),
        P("dp"),
    )
    return jax.shard_map(
        body,
        mesh=mesh,
        in_specs=placed,
        out_specs=(P("dp", "tp"), P("dp", None, None)),
        check_vma=False,
    )
```

```python
import math

import jax
import jax.numpy as jnp
from jax import lax
from jax.experimental import pallas as pl
from jax.experimental.pallas import tpu as pltpu
from jax.sharding import PartitionSpec as P

softmax_scale = 192.0 ** (-0.5) * (0.1 * math.log(40.0) + 1.0) ** 2

GROUP = 512
BLOCK = 128
TILES = 5
MAIN = 8
REST = 2
CAP = 10
F32 = jnp.float32
BF16 = jnp.bfloat16
SWAP = ((0, 1), (1, 0))
HBM = pl.BlockSpec(memory_space=pl.ANY)
VMEM = pl.BlockSpec(memory_space=pltpu.VMEM)
SMEM = pl.BlockSpec(memory_space=pltpu.SMEM)
PARAMS = pltpu.CompilerParams(vmem_limit_bytes=58 * 1024 * 1024)


def dot(a, b):
    return jnp.dot(a, b, preferred_element_type=F32)


def iota(shape, dim):
    return lax.broadcasted_iota(jnp.int32, shape, dim)


def one_hot(a, b):
    return (a == b).astype(F32).astype(BF16)


def groups_of(features):
    blocks = features // BLOCK
    return [(at * BLOCK, min(4, blocks - at), at // 4 * TILES) for at in range(0, blocks, 4)]


def tiles_in(features):
    return sum(blocks + 1 for _, blocks, _ in groups_of(features))


def back_groups(features):
    half = features // 2
    shift = tiles_in(half)
    return [(h * half + at, blocks, h * shift + t) for h in range(2) for at, blocks, t in groups_of(half)]


def pack_copies(packed, messages, sems, groups):
    copies = []
    for g, (_, blocks, tile) in enumerate(groups):
        for i, part in enumerate((pl.ds(tile, blocks), pl.ds(tile + blocks, 1))):
            copies.append(pltpu.make_async_copy(packed.at[:, part], messages.at[:, part], sems.at[2 * g + i]))
    return copies


def start(copies):
    for each in copies:
        each.start()


def wait(copies):
    for each in copies:
        each.wait()


def features_of(group):
    return slice(group * GROUP, (group + 1) * GROUP)


def block_of(f):
    return slice(f * BLOCK, (f + 1) * BLOCK)


def unit_of(row, half):
    return ((row & (2 * half - 1)) >> 1) * MAIN + lax.div(row, 2 * half) * REST + (row & 1)


def fill_place(ref, dp_count):
    size = ref.shape[0]
    ref[...] = one_hot(iota((size, size), 0), unit_of(iota((size, size), 1), dp_count // 2))


def fill_pick(ref, dp_count):
    size = ref.shape[0]
    ref[...] = one_hot(iota((size, size), 1), unit_of(iota((size, size), 0), dp_count // 2))


def pack(value, ref, tile):
    dp_count = ref.shape[0]
    blocks = value.shape[1] // BLOCK
    main, half = dp_count * MAIN, dp_count // 2
    for f in range(blocks):
        part = value[:main, block_of(f)].astype(BF16)
        ref[:, tile + f] = part.reshape(dp_count, MAIN, BLOCK)
    rest = value[main:].astype(BF16)
    empty = [jnp.zeros((2 * half, BLOCK), BF16)] * (4 - blocks)
    sides = [rest[: 2 * half], rest[2 * half :]]
    sides = [jnp.concatenate([side[:, block_of(f)] for f in range(blocks)] + empty, axis=0) for side in sides]
    return jnp.concatenate(sides, axis=1)


def place_rest(rest, place, ref, tile):
    half = ref.shape[0] // 2
    rest = dot(place, rest)
    for h in range(2):
        part = rest[:, block_of(h)].astype(BF16)
        ref[h * half : (h + 1) * half, tile] = part.reshape(half, MAIN, BLOCK)


def pack_all(groups, value_of, place, packed, copies):
    rest, last = None, 0
    for g, (at, blocks, tile) in enumerate(groups):
        value = value_of(slice(at, at + blocks * BLOCK))
        if g:
            place_rest(rest, place, packed, last)
        rest, last = pack(value, packed, tile), tile + blocks
        start([copies[2 * g]] + ([copies[2 * g - 1]] if g else []))
    place_rest(rest, place, packed, last)
    start(copies[-1:])
    wait(copies)


def pick_rest(ref, pick, tile):
    dp_count = ref.shape[0]
    main, half = dp_count * MAIN, dp_count // 2
    rest = ref[:, tile].reshape(main, BLOCK)
    rest = dot(pick, jnp.concatenate([rest[: main // 2], rest[main // 2 :]], axis=1)).astype(BF16)
    sides = [
        jnp.concatenate([rest[2 * half * f : 2 * half * (f + 1), block_of(h)] for f in range(4)], axis=1)
        for h in range(2)
    ]
    return jnp.concatenate(sides, axis=0)


def main_rows(ref, tile, blocks):
    main = ref.shape[0] * MAIN
    return jnp.concatenate([ref[:, tile + f].reshape(main, BLOCK) for f in range(blocks)], axis=1)


def row_of(index, dp_count):
    main = dp_count * MAIN
    first = index < main
    after = index - main
    return jnp.where(first, index >> 3, after >> 1), jnp.where(first, index & 7, MAIN + (after & 1))


def rank_code(routes):
    top, tokens = routes.shape
    slots = iota((128, tokens), 0)
    named = jnp.zeros((128, tokens), F32)
    for k in range(top):
        named = named + (routes[k : k + 1] == slots).astype(F32)
    earlier = (iota((tokens, tokens), 0) < iota((tokens, tokens), 1)).astype(F32).astype(BF16)
    rank = dot(named.astype(BF16), earlier)
    return jnp.where(named > 0.0, rank, -1.0)


def dispatch_kernel(
    core_ref, routes_ref, tokens_ref, out_ref, routes, rows, chosen, place, packed, in_sem, out_sem
):
    dp_count = out_ref.shape[0]
    groups = out_ref.shape[1] // TILES
    loads = [
        pltpu.make_async_copy(tokens_ref.at[:, features_of(g)], rows.at[:, features_of(g)], in_sem.at[g])
        for g in range(groups)
    ]
    routes_load = pltpu.make_async_copy(routes_ref, routes, in_sem.at[groups])
    start([routes_load] + loads)
    fill_place(place, dp_count)
    wait([routes_load])
    code = rank_code(routes[...]).astype(BF16)
    tokens = code.shape[1]
    count = dp_count * CAP
    owner, _ = row_of(iota((count, 128), 0), dp_count)
    spread = dot(one_hot(iota((count, 128), 1), 2 * owner + core_ref[0]), code)
    _, turn = row_of(iota((count, tokens), 0), dp_count)
    chosen[...] = one_hot(spread, turn.astype(F32))
    wait(loads)
    parts = groups_of(rows.shape[1])
    stores = pack_copies(packed, out_ref, out_sem, parts)
    pack_all(parts, lambda part: dot(chosen[...], rows[:, part]), place[...], packed, stores)


def dispatch(core, routes, tokens, dp_count):
    count, features = tokens.shape
    groups = features // GROUP
    shape = (dp_count, TILES * groups, MAIN, BLOCK)
    return pl.pallas_call(
        dispatch_kernel,
        in_specs=[SMEM, HBM, HBM],
        out_specs=HBM,
        out_shape=jax.ShapeDtypeStruct(shape, BF16),
        scratch_shapes=[
            pltpu.VMEM(routes.shape, jnp.int32),
            pltpu.VMEM(tokens.shape, BF16),
            pltpu.VMEM((dp_count * CAP, count), BF16),
            pltpu.VMEM((4 * dp_count, 4 * dp_count), BF16),
            pltpu.VMEM(shape, BF16),
            pltpu.SemaphoreType.DMA((groups + 1,)),
            pltpu.SemaphoreType.DMA((2 * groups,)),
        ],
        compiler_params=PARAMS,
        name="dispatch",
    )(core, routes, tokens)


def stages_of(groups):
    edges = [0, 1] + list(range(3, groups, 2)) + [groups]
    return list(zip(edges[:-1], edges[1:]))


def expert_kernel(
    core_ref,
    message_ref,
    in_own_ref,
    up_own_ref,
    in_far_ref,
    up_far_ref,
    out_own_ref,
    out_far_ref,
    back_ref,
    message,
    rows,
    in_own,
    up_own,
    in_far,
    up_far,
    out_both,
    gate_sum,
    up_sum,
    hidden,
    packed,
    pick,
    place,
    message_sem,
    weight_sem,
    far_sem,
    back_sem,
):
    core = core_ref[0]
    dp_count = message.shape[0]
    groups = message.shape[1] // TILES
    width = in_own.shape[1]
    stages = stages_of(groups)
    copy = pltpu.make_async_copy

    def stage_copies(i):
        first, last = stages[i]
        part = pl.ds(first * GROUP, (last - first) * GROUP)
        return [
            copy(in_own_ref.at[core, part], in_own.at[part], weight_sem.at[2 * i]),
            copy(up_own_ref.at[core, part], up_own.at[part], weight_sem.at[2 * i + 1]),
        ]

    def message_copy(i):
        first, last = stages[i]
        part = pl.ds(first * TILES, (last - first) * TILES)
        return copy(message_ref.at[:, part], message.at[:, part], message_sem.at[i])

    def unpack(i):
        for g in range(*stages[i]):
            rows[: dp_count * MAIN, features_of(g)] = main_rows(message, g * TILES, 4)
            rows[dp_count * MAIN :, features_of(g)] = pick_rest(message, pick[...], g * TILES + 4)

    far_copies = [
        copy(in_far_ref, in_far, far_sem.at[0]),
        copy(up_far_ref, up_far, far_sem.at[1]),
        copy(out_own_ref.at[core], out_both.at[pl.ds(0, width)], far_sem.at[2]),
        copy(out_far_ref, out_both.at[pl.ds(width, width)], far_sem.at[3]),
    ]
    staged = [stage_copies(i) for i in range(len(stages))] + [far_copies[:2], far_copies[2:]]
    messages = [message_copy(i) for i in range(len(stages))]
    parts = back_groups(rows.shape[1])
    back_copies = pack_copies(packed, back_ref, back_sem, parts)
    start(messages + staged[0] + staged[1] + staged[2])
    fill_pick(pick, dp_count)
    fill_place(place, dp_count)
    wait(messages[:1])
    unpack(0)

    for i, (first, last) in enumerate(stages):
        wait(staged[i])
        if i + 3 < len(staged):
            start(staged[i + 3])
        if 0 < i < len(stages) - 1:
            wait([messages[i + 1]])
            unpack(i + 1)
        part = slice(first * GROUP, last * GROUP)
        gate = dot(rows[:, part], in_own[part])
        up = dot(rows[:, part], up_own[part])
        if i > 0:
            gate = gate + gate_sum[...]
            up = up + up_sum[...]
        if i + 1 < len(stages):
            gate_sum[...] = gate
            up_sum[...] = up
        else:
            hidden[:, :width] = (gate / (1.0 + jnp.exp(-gate)) * up).astype(BF16)
        if i == 0:
            wait([messages[1]])
            unpack(1)
    wait(far_copies[:2])
    gate = dot(rows[...], in_far[...])
    up = dot(rows[...], up_far[...])
    hidden[:, width:] = (gate / (1.0 + jnp.exp(-gate)) * up).astype(BF16)
    wait(far_copies[2:])
    pack_all(parts, lambda part: dot(hidden[...], out_both[:, part]), place[...], packed, back_copies)


def experts(core, message, w_in, w_up, w_out, in_far, up_far, out_far):
    dp_count, tiles = message.shape[:2]
    groups = tiles // TILES
    features, width = in_far.shape
    count = dp_count * CAP
    stages = len(stages_of(groups))
    back = (dp_count, 2 * tiles_in(features // 2), MAIN, BLOCK)
    weight = pltpu.VMEM((features, width), BF16)
    total = pltpu.VMEM((count, width), F32)
    square = pltpu.VMEM((4 * dp_count, 4 * dp_count), BF16)
    return pl.pallas_call(
        expert_kernel,
        in_specs=[SMEM] + [HBM] * 7,
        out_specs=HBM,
        out_shape=jax.ShapeDtypeStruct(back, BF16),
        scratch_shapes=[
            pltpu.VMEM(message.shape, BF16),
            pltpu.VMEM((count, features), BF16),
            weight,
            weight,
            weight,
            weight,
            pltpu.VMEM((2 * width, features), BF16),
            total,
            total,
            pltpu.VMEM((count, 2 * width), BF16),
            pltpu.VMEM(back, BF16),
            square,
            square,
            pltpu.SemaphoreType.DMA((stages,)),
            pltpu.SemaphoreType.DMA((2 * stages,)),
            pltpu.SemaphoreType.DMA((4,)),
            pltpu.SemaphoreType.DMA((2 * len(back_groups(features)),)),
        ],
        compiler_params=PARAMS,
        cost_estimate=pl.CostEstimate(
            flops=12 * count * features * width, bytes_accessed=32 * 1024 * 1024, transcendentals=0
        ),
        name="experts",
    )(core, message, w_in, w_up, in_far, up_far, w_out, out_far)


def spread_gates(core, routes, gates, count):
    top, tokens = routes.shape
    dp_count = count // CAP
    code = rank_code(routes).astype(BF16)
    slots = iota((128, tokens), 0)
    value = jnp.zeros((128, tokens), F32)
    for k in range(top):
        value = value + jnp.where(routes[k : k + 1] == slots, gates[k : k + 1], 0.0)
    high = value.astype(BF16)
    low = (value - high.astype(F32)).astype(BF16)
    owner, _ = row_of(iota((128, count), 1), dp_count)
    owner = one_hot(iota((128, count), 0), 2 * owner + core)
    _, turn = row_of(iota((tokens, count), 1), dp_count)
    here = dot(code.T, owner) == turn.astype(F32)
    parts = [jnp.where(here, dot(source.T, owner), 0.0) for source in (high, low)]
    return jnp.concatenate(parts, axis=0).astype(BF16)


def combine_kernel(
    back_ref, routes_ref, gates_ref, after_ref, out_ref, message, routes, gates, spread, total, pick, sem, out_sem
):
    dp_count = message.shape[0]
    tiles = message.shape[1] // 2
    count = dp_count * CAP
    tokens = total.shape[0]
    parts = groups_of(total.shape[1])
    loads, stores = [], []
    for g, (at, blocks, tile) in enumerate(parts):
        lanes = slice(at, at + blocks * BLOCK)
        stores.append(pltpu.make_async_copy(total.at[:, lanes], out_ref.at[:, lanes], out_sem.at[g]))
        for core in range(2):
            part = pl.ds(core * tiles + tile, blocks + 1)
            loads.append(pltpu.make_async_copy(back_ref.at[:, part], message.at[:, part], sem.at[2 * g + core]))
    first = [
        pltpu.make_async_copy(routes_ref, routes, sem.at[len(loads)]),
        pltpu.make_async_copy(gates_ref, gates, sem.at[len(loads) + 1]),
    ]
    start(first + loads)
    fill_pick(pick, dp_count)
    wait(first)
    for core in range(2):
        spread[:, core * count : (core + 1) * count] = spread_gates(core, routes[...], gates[...], count)

    def picked(g):
        _, blocks, tile = parts[g]
        return [pick_rest(message, pick[...], core * tiles + tile + blocks) for core in range(2)]

    wait(loads[:2])
    rest = picked(0)
    for g, (at, blocks, tile) in enumerate(parts):
        wait(loads[2 * g + 2 : 2 * g + 4])
        rows = []
        for core in range(2):
            rows += [main_rows(message, core * tiles + tile, blocks), rest[core][:, : blocks * BLOCK]]
        value = dot(spread[...], jnp.concatenate(rows, axis=0))
        if g + 1 < len(parts):
            rest = picked(g + 1)
        total[:, at : at + blocks * BLOCK] = (value[:tokens] + value[tokens:]).astype(BF16)
        start(stores[g : g + 1])
    wait(stores)


def combine(back, routes, gates, after):
    dp_count, tiles = back.shape[0], back.shape[1]
    tokens = routes.shape[1]
    blocks = tiles // 2 - -(-(tiles // 2) // TILES)
    parts = len(groups_of(blocks * BLOCK))
    out = jax.ShapeDtypeStruct((tokens, blocks * BLOCK), BF16)
    return pl.pallas_call(
        combine_kernel,
        in_specs=[HBM, HBM, HBM, HBM],
        out_specs=HBM,
        out_shape=out,
        scratch_shapes=[
            pltpu.VMEM(back.shape, BF16),
            pltpu.VMEM(routes.shape, jnp.int32),
            pltpu.VMEM(gates.shape, F32),
            pltpu.VMEM((2 * tokens, 2 * dp_count * CAP), BF16),
            pltpu.VMEM(out.shape, BF16),
            pltpu.VMEM((4 * dp_count, 4 * dp_count), BF16),
            pltpu.SemaphoreType.DMA((2 * parts + 2,)),
            pltpu.SemaphoreType.DMA((parts,)),
        ],
        compiler_params=PARAMS,
        name="combine",
    )(back, routes, gates, after)


def attention(query_latent, query_rope, cache_latent, cache_rope, lengths):
    local_span = cache_latent.shape[1]
    positions = lax.axis_index("tp") * local_span + jnp.arange(local_span, dtype=jnp.int32)
    visible = positions[None, None, :] < lengths[:, None, None]
    scores = (
        jnp.einsum("bhl,btl->bht", query_latent, cache_latent, preferred_element_type=F32)
        + jnp.einsum("bhr,brt->bht", query_rope, cache_rope, preferred_element_type=F32)
    ) * softmax_scale
    peak = jnp.max(jnp.where(visible, scores, -1e30), axis=2, keepdims=True)
    weights = jnp.where(visible, jnp.exp(scores - peak), 0.0)
    total = jnp.sum(weights, axis=2, keepdims=True)
    numer = jnp.einsum("bht,btl->bhl", weights.astype(BF16), cache_latent, preferred_element_type=F32)
    both = jnp.concatenate(
        [numer, jnp.broadcast_to(total, total.shape[:2] + (64,)), jnp.broadcast_to(peak, peak.shape[:2] + (64,))],
        axis=2,
    )
    far = lax.ppermute(both, "tp", SWAP)
    lat = numer.shape[2]
    far_numer, far_total, far_peak = far[:, :, :lat], far[:, :, lat : lat + 1], far[:, :, lat + 64 : lat + 65]
    top = jnp.maximum(peak, far_peak)
    here, there = jnp.exp(peak - top), jnp.exp(far_peak - top)
    return ((numer * here + far_numer * there) / (total * here + far_total * there)).astype(BF16)


def body(
    moe_tokens,
    slot_routes,
    route_gates,
    w_in,
    w_up,
    w_out,
    query_latent,
    query_rope,
    cache_latent,
    cache_rope,
    lengths,
):
    dp_count = lax.axis_size("dp")
    index = lax.axis_index("tp")
    core = jnp.reshape(index, (1,)).astype(jnp.int32)
    routes = slot_routes.T
    outbound = dispatch(core, routes, moe_tokens, dp_count)
    message = lax.all_to_all(outbound, "dp", split_axis=0, concat_axis=0, tiled=True)

    def swap(weight):
        return lax.ppermute(lax.dynamic_index_in_dim(weight, 1 - index, 0, False), "tp", SWAP)

    in_far, up_far, out_far = swap(w_in), swap(w_up), swap(w_out)
    back = experts(core, message, w_in, w_up, w_out, in_far, up_far, out_far)
    parts = back.shape
    back = back.reshape(2 * parts[0], parts[1] // 2, MAIN, BLOCK)
    returned = lax.all_to_all(back, ("dp", "tp"), split_axis=0, concat_axis=0, tiled=True)
    attn_out = attention(query_latent, query_rope, cache_latent, cache_rope, lengths)
    moe_out = combine(returned.reshape(parts), routes, route_gates.T, attn_out)
    return (moe_out, attn_out)


def solution(mesh):
    placed = (
        P("dp", None),
        P("dp", None),
        P("dp", None),
        P("dp", None, "tp"),
        P("dp", None, "tp"),
        P("dp", "tp", None),
        P("dp", None, None),
        P("dp", None, None),
        P("dp", "tp", None),
        P("dp", None, "tp"),
        P("dp"),
    )
    return jax.shard_map(
        body,
        mesh=mesh,
        in_specs=placed,
        out_specs=(P("dp", "tp"), P("dp", None, None)),
        check_vma=False,
    )
```

```python
import math

import jax
import jax.numpy as jnp
from jax import lax
from jax.experimental import pallas as pl
from jax.experimental.pallas import tpu as pltpu
from jax.sharding import PartitionSpec as P

softmax_scale = 192.0 ** (-0.5) * (0.1 * math.log(40.0) + 1.0) ** 2

GROUP = 512
BLOCK = 128
TILES = 5
MAIN = 8
REST = 2
CAP = 10
F32 = jnp.float32
BF16 = jnp.bfloat16
SWAP = ((0, 1), (1, 0))
HBM = pl.BlockSpec(memory_space=pl.ANY)
VMEM = pl.BlockSpec(memory_space=pltpu.VMEM)
SMEM = pl.BlockSpec(memory_space=pltpu.SMEM)
PARAMS = pltpu.CompilerParams(vmem_limit_bytes=58 * 1024 * 1024)


def dot(a, b):
    return jnp.dot(a, b, preferred_element_type=F32)


def iota(shape, dim):
    return lax.broadcasted_iota(jnp.int32, shape, dim)


def one_hot(a, b):
    return (a == b).astype(F32).astype(BF16)


def groups_of(features):
    blocks = features // BLOCK
    return [(at * BLOCK, min(4, blocks - at), at // 4 * TILES) for at in range(0, blocks, 4)]


def tiles_in(features):
    return sum(blocks + 1 for _, blocks, _ in groups_of(features))


def back_groups(features):
    half = features // 2
    shift = tiles_in(half)
    return [(h * half + at, blocks, h * shift + t) for h in range(2) for at, blocks, t in groups_of(half)]


def pack_copies(packed, messages, sems, groups):
    copies = []
    for g, (_, blocks, tile) in enumerate(groups):
        for i, part in enumerate((pl.ds(tile, blocks), pl.ds(tile + blocks, 1))):
            copies.append(pltpu.make_async_copy(packed.at[:, part], messages.at[:, part], sems.at[2 * g + i]))
    return copies


def start(copies):
    for each in copies:
        each.start()


def wait(copies):
    for each in copies:
        each.wait()


def features_of(group):
    return slice(group * GROUP, (group + 1) * GROUP)


def block_of(f):
    return slice(f * BLOCK, (f + 1) * BLOCK)


def unit_of(row, half):
    return ((row & (2 * half - 1)) >> 1) * MAIN + lax.div(row, 2 * half) * REST + (row & 1)


def fill_place(ref, dp_count):
    size = ref.shape[0]
    ref[...] = one_hot(iota((size, size), 0), unit_of(iota((size, size), 1), dp_count // 2))


def fill_pick(ref, dp_count):
    size = ref.shape[0]
    ref[...] = one_hot(iota((size, size), 1), unit_of(iota((size, size), 0), dp_count // 2))


def pack(value, ref, tile):
    dp_count = ref.shape[0]
    blocks = value.shape[1] // BLOCK
    main, half = dp_count * MAIN, dp_count // 2
    for f in range(blocks):
        part = value[:main, block_of(f)].astype(BF16)
        ref[:, tile + f] = part.reshape(dp_count, MAIN, BLOCK)
    rest = value[main:].astype(BF16)
    empty = [jnp.zeros((2 * half, BLOCK), BF16)] * (4 - blocks)
    sides = [rest[: 2 * half], rest[2 * half :]]
    sides = [jnp.concatenate([side[:, block_of(f)] for f in range(blocks)] + empty, axis=0) for side in sides]
    return jnp.concatenate(sides, axis=1)


def place_rest(rest, place, ref, tile):
    half = ref.shape[0] // 2
    rest = dot(place, rest)
    for h in range(2):
        part = rest[:, block_of(h)].astype(BF16)
        ref[h * half : (h + 1) * half, tile] = part.reshape(half, MAIN, BLOCK)


def pack_all(groups, value_of, place, packed, copies):
    rest, last = None, 0
    for g, (at, blocks, tile) in enumerate(groups):
        value = value_of(slice(at, at + blocks * BLOCK))
        if g:
            place_rest(rest, place, packed, last)
        rest, last = pack(value, packed, tile), tile + blocks
        start([copies[2 * g]] + ([copies[2 * g - 1]] if g else []))
    place_rest(rest, place, packed, last)
    start(copies[-1:])
    wait(copies)


def pick_rest(ref, pick, tile):
    dp_count = ref.shape[0]
    main, half = dp_count * MAIN, dp_count // 2
    rest = ref[:, tile].reshape(main, BLOCK)
    rest = dot(pick, jnp.concatenate([rest[: main // 2], rest[main // 2 :]], axis=1)).astype(BF16)
    sides = [
        jnp.concatenate([rest[2 * half * f : 2 * half * (f + 1), block_of(h)] for f in range(4)], axis=1)
        for h in range(2)
    ]
    return jnp.concatenate(sides, axis=0)


def main_rows(ref, tile, blocks):
    main = ref.shape[0] * MAIN
    return jnp.concatenate([ref[:, tile + f].reshape(main, BLOCK) for f in range(blocks)], axis=1)


def row_of(index, dp_count):
    main = dp_count * MAIN
    first = index < main
    after = index - main
    return jnp.where(first, index >> 3, after >> 1), jnp.where(first, index & 7, MAIN + (after & 1))


def rank_code(routes):
    top, tokens = routes.shape
    slots = iota((128, tokens), 0)
    named = jnp.zeros((128, tokens), F32)
    for k in range(top):
        named = named + (routes[k : k + 1] == slots).astype(F32)
    earlier = (iota((tokens, tokens), 0) < iota((tokens, tokens), 1)).astype(F32).astype(BF16)
    rank = dot(named.astype(BF16), earlier)
    return jnp.where(named > 0.0, rank, -1.0)


def dispatch_kernel(
    core_ref, routes_ref, tokens_ref, out_ref, routes, rows, chosen, place, packed, in_sem, out_sem
):
    dp_count = out_ref.shape[0]
    groups = out_ref.shape[1] // TILES
    loads = [
        pltpu.make_async_copy(tokens_ref.at[:, features_of(g)], rows.at[:, features_of(g)], in_sem.at[g])
        for g in range(groups)
    ]
    routes_load = pltpu.make_async_copy(routes_ref, routes, in_sem.at[groups])
    start([routes_load] + loads)
    fill_place(place, dp_count)
    wait([routes_load])
    code = rank_code(routes[...]).astype(BF16)
    tokens = code.shape[1]
    count = dp_count * CAP
    owner, _ = row_of(iota((count, 128), 0), dp_count)
    spread = dot(one_hot(iota((count, 128), 1), 2 * owner + core_ref[0]), code)
    _, turn = row_of(iota((count, tokens), 0), dp_count)
    chosen[...] = one_hot(spread, turn.astype(F32))
    wait(loads)
    parts = groups_of(rows.shape[1])
    stores = pack_copies(packed, out_ref, out_sem, parts)
    pack_all(parts, lambda part: dot(chosen[...], rows[:, part]), place[...], packed, stores)


def dispatch(core, routes, tokens, dp_count):
    count, features = tokens.shape
    groups = features // GROUP
    shape = (dp_count, TILES * groups, MAIN, BLOCK)
    return pl.pallas_call(
        dispatch_kernel,
        in_specs=[SMEM, HBM, HBM],
        out_specs=HBM,
        out_shape=jax.ShapeDtypeStruct(shape, BF16),
        scratch_shapes=[
            pltpu.VMEM(routes.shape, jnp.int32),
            pltpu.VMEM(tokens.shape, BF16),
            pltpu.VMEM((dp_count * CAP, count), BF16),
            pltpu.VMEM((4 * dp_count, 4 * dp_count), BF16),
            pltpu.VMEM(shape, BF16),
            pltpu.SemaphoreType.DMA((groups + 1,)),
            pltpu.SemaphoreType.DMA((2 * groups,)),
        ],
        compiler_params=PARAMS,
        name="dispatch",
    )(core, routes, tokens)


def stages_of(groups):
    edges = [0, 1] + list(range(3, groups, 2)) + [groups]
    return list(zip(edges[:-1], edges[1:]))


def expert_kernel(
    core_ref,
    message_ref,
    in_own_ref,
    up_own_ref,
    in_far_ref,
    up_far_ref,
    out_own_ref,
    out_far_ref,
    back_ref,
    message,
    rows,
    in_own,
    up_own,
    in_far,
    up_far,
    out_both,
    gate_sum,
    up_sum,
    hidden,
    packed,
    pick,
    place,
    message_sem,
    weight_sem,
    far_sem,
    back_sem,
):
    core = core_ref[0]
    dp_count = message.shape[0]
    groups = message.shape[1] // TILES
    width = in_own.shape[1]
    stages = stages_of(groups)
    copy = pltpu.make_async_copy

    def stage_copies(i):
        first, last = stages[i]
        part = pl.ds(first * GROUP, (last - first) * GROUP)
        return [
            copy(in_own_ref.at[core, part], in_own.at[part], weight_sem.at[2 * i]),
            copy(up_own_ref.at[core, part], up_own.at[part], weight_sem.at[2 * i + 1]),
        ]

    def message_copy(i):
        first, last = stages[i]
        part = pl.ds(first * TILES, (last - first) * TILES)
        return copy(message_ref.at[:, part], message.at[:, part], message_sem.at[i])

    def unpack(i):
        for g in range(*stages[i]):
            rows[: dp_count * MAIN, features_of(g)] = main_rows(message, g * TILES, 4)
            rows[dp_count * MAIN :, features_of(g)] = pick_rest(message, pick[...], g * TILES + 4)

    far_copies = [
        copy(in_far_ref, in_far, far_sem.at[0]),
        copy(up_far_ref, up_far, far_sem.at[1]),
        copy(out_own_ref.at[core], out_both.at[pl.ds(0, width)], far_sem.at[2]),
        copy(out_far_ref, out_both.at[pl.ds(width, width)], far_sem.at[3]),
    ]
    staged = [stage_copies(i) for i in range(len(stages))] + [far_copies[:2], far_copies[2:]]
    messages = [message_copy(i) for i in range(len(stages))]
    parts = back_groups(rows.shape[1])
    back_copies = pack_copies(packed, back_ref, back_sem, parts)
    start(messages + staged[0] + staged[1] + staged[2])
    fill_pick(pick, dp_count)
    fill_place(place, dp_count)
    wait(messages[:1])
    unpack(0)

    for i, (first, last) in enumerate(stages):
        wait(staged[i])
        if i + 3 < len(staged):
            start(staged[i + 3])
        if 0 < i < len(stages) - 1:
            wait([messages[i + 1]])
            unpack(i + 1)
        part = slice(first * GROUP, last * GROUP)
        gate = dot(rows[:, part], in_own[part])
        up = dot(rows[:, part], up_own[part])
        if i > 0:
            gate = gate + gate_sum[...]
            up = up + up_sum[...]
        if i + 1 < len(stages):
            gate_sum[...] = gate
            up_sum[...] = up
        else:
            hidden[:, :width] = (gate / (1.0 + jnp.exp(-gate)) * up).astype(BF16)
        if i == 0:
            wait([messages[1]])
            unpack(1)
    wait(far_copies[:2])
    gate = dot(rows[...], in_far[...])
    up = dot(rows[...], up_far[...])
    hidden[:, width:] = (gate / (1.0 + jnp.exp(-gate)) * up).astype(BF16)
    wait(far_copies[2:])
    pack_all(parts, lambda part: dot(hidden[...], out_both[:, part]), place[...], packed, back_copies)


def experts(core, message, w_in, w_up, w_out, in_far, up_far, out_far):
    dp_count, tiles = message.shape[:2]
    groups = tiles // TILES
    features, width = in_far.shape
    count = dp_count * CAP
    stages = len(stages_of(groups))
    back = (dp_count, 2 * tiles_in(features // 2), MAIN, BLOCK)
    weight = pltpu.VMEM((features, width), BF16)
    total = pltpu.VMEM((count, width), F32)
    square = pltpu.VMEM((4 * dp_count, 4 * dp_count), BF16)
    return pl.pallas_call(
        expert_kernel,
        in_specs=[SMEM] + [HBM] * 7,
        out_specs=HBM,
        out_shape=jax.ShapeDtypeStruct(back, BF16),
        scratch_shapes=[
            pltpu.VMEM(message.shape, BF16),
            pltpu.VMEM((count, features), BF16),
            weight,
            weight,
            weight,
            weight,
            pltpu.VMEM((2 * width, features), BF16),
            total,
            total,
            pltpu.VMEM((count, 2 * width), BF16),
            pltpu.VMEM(back, BF16),
            square,
            square,
            pltpu.SemaphoreType.DMA((stages,)),
            pltpu.SemaphoreType.DMA((2 * stages,)),
            pltpu.SemaphoreType.DMA((4,)),
            pltpu.SemaphoreType.DMA((2 * len(back_groups(features)),)),
        ],
        compiler_params=PARAMS,
        cost_estimate=pl.CostEstimate(
            flops=12 * count * features * width, bytes_accessed=32 * 1024 * 1024, transcendentals=0
        ),
        name="experts",
    )(core, message, w_in, w_up, in_far, up_far, w_out, out_far)


def spread_gates(core, routes, gates, count):
    top, tokens = routes.shape
    dp_count = count // CAP
    code = rank_code(routes).astype(BF16)
    slots = iota((128, tokens), 0)
    value = jnp.zeros((128, tokens), F32)
    for k in range(top):
        value = value + jnp.where(routes[k : k + 1] == slots, gates[k : k + 1], 0.0)
    high = value.astype(BF16)
    low = (value - high.astype(F32)).astype(BF16)
    owner, _ = row_of(iota((128, count), 1), dp_count)
    owner = one_hot(iota((128, count), 0), 2 * owner + core)
    _, turn = row_of(iota((tokens, count), 1), dp_count)
    here = dot(code.T, owner) == turn.astype(F32)
    parts = [jnp.where(here, dot(source.T, owner), 0.0) for source in (high, low)]
    return jnp.concatenate(parts, axis=0).astype(BF16)


def gates_kernel(routes_ref, gates_ref, out_ref):
    count = out_ref.shape[1] // 2
    for core in range(2):
        out_ref[:, core * count : (core + 1) * count] = spread_gates(core, routes_ref[...], gates_ref[...], count)


def gate_matrix(routes, gates, dp_count):
    return pl.pallas_call(
        gates_kernel,
        in_specs=[VMEM, VMEM],
        out_specs=VMEM,
        out_shape=jax.ShapeDtypeStruct((2 * routes.shape[1], 2 * dp_count * CAP), BF16),
        compiler_params=PARAMS,
        name="gates",
    )(routes, gates)


def combine_kernel(back_ref, gates_ref, after_ref, out_ref, message, spread, total, pick, sem, out_sem):
    dp_count = message.shape[0]
    tiles = message.shape[1] // 2
    tokens = total.shape[0]
    parts = groups_of(total.shape[1])
    loads, stores = [], []
    for g, (at, blocks, tile) in enumerate(parts):
        lanes = slice(at, at + blocks * BLOCK)
        stores.append(pltpu.make_async_copy(total.at[:, lanes], out_ref.at[:, lanes], out_sem.at[g]))
        for core in range(2):
            part = pl.ds(core * tiles + tile, blocks + 1)
            loads.append(pltpu.make_async_copy(back_ref.at[:, part], message.at[:, part], sem.at[2 * g + core]))
    gates_load = pltpu.make_async_copy(gates_ref, spread, sem.at[len(loads)])
    start(loads[:2] + [gates_load] + loads[2:])
    fill_pick(pick, dp_count)

    def picked(g):
        _, blocks, tile = parts[g]
        return [pick_rest(message, pick[...], core * tiles + tile + blocks) for core in range(2)]

    wait(loads[:2])
    rest = picked(0)
    wait([gates_load])
    for g, (at, blocks, tile) in enumerate(parts):
        wait(loads[2 * g + 2 : 2 * g + 4])
        rows = []
        for core in range(2):
            rows += [main_rows(message, core * tiles + tile, blocks), rest[core][:, : blocks * BLOCK]]
        value = dot(spread[...], jnp.concatenate(rows, axis=0))
        if g + 1 < len(parts):
            rest = picked(g + 1)
        total[:, at : at + blocks * BLOCK] = (value[:tokens] + value[tokens:]).astype(BF16)
        start(stores[g : g + 1])
    wait(stores)


def combine(back, gates, after):
    dp_count, tiles = back.shape[0], back.shape[1]
    tokens = gates.shape[0] // 2
    blocks = tiles // 2 - -(-(tiles // 2) // TILES)
    parts = len(groups_of(blocks * BLOCK))
    out = jax.ShapeDtypeStruct((tokens, blocks * BLOCK), BF16)
    return pl.pallas_call(
        combine_kernel,
        in_specs=[HBM, HBM, HBM],
        out_specs=HBM,
        out_shape=out,
        scratch_shapes=[
            pltpu.VMEM(back.shape, BF16),
            pltpu.VMEM(gates.shape, BF16),
            pltpu.VMEM(out.shape, BF16),
            pltpu.VMEM((4 * dp_count, 4 * dp_count), BF16),
            pltpu.SemaphoreType.DMA((2 * parts + 1,)),
            pltpu.SemaphoreType.DMA((parts,)),
        ],
        compiler_params=PARAMS,
        name="combine",
    )(back, gates, after)


def attention(query_latent, query_rope, cache_latent, cache_rope, lengths):
    local_span = cache_latent.shape[1]
    positions = lax.axis_index("tp") * local_span + jnp.arange(local_span, dtype=jnp.int32)
    visible = positions[None, None, :] < lengths[:, None, None]
    scores = (
        jnp.einsum("bhl,btl->bht", query_latent, cache_latent, preferred_element_type=F32)
        + jnp.einsum("bhr,brt->bht", query_rope, cache_rope, preferred_element_type=F32)
    ) * softmax_scale
    peak = jnp.max(jnp.where(visible, scores, -1e30), axis=2, keepdims=True)
    weights = jnp.where(visible, jnp.exp(scores - peak), 0.0)
    total = jnp.sum(weights, axis=2, keepdims=True)
    numer = jnp.einsum("bht,btl->bhl", weights.astype(BF16), cache_latent, preferred_element_type=F32)
    both = jnp.concatenate(
        [numer, jnp.broadcast_to(total, total.shape[:2] + (64,)), jnp.broadcast_to(peak, peak.shape[:2] + (64,))],
        axis=2,
    )
    far = lax.ppermute(both, "tp", SWAP)
    lat = numer.shape[2]
    far_numer, far_total, far_peak = far[:, :, :lat], far[:, :, lat : lat + 1], far[:, :, lat + 64 : lat + 65]
    top = jnp.maximum(peak, far_peak)
    here, there = jnp.exp(peak - top), jnp.exp(far_peak - top)
    return ((numer * here + far_numer * there) / (total * here + far_total * there)).astype(BF16)


def body(
    moe_tokens,
    slot_routes,
    route_gates,
    w_in,
    w_up,
    w_out,
    query_latent,
    query_rope,
    cache_latent,
    cache_rope,
    lengths,
):
    dp_count = lax.axis_size("dp")
    index = lax.axis_index("tp")
    core = jnp.reshape(index, (1,)).astype(jnp.int32)
    routes = slot_routes.T
    outbound = dispatch(core, routes, moe_tokens, dp_count)
    message = lax.all_to_all(outbound, "dp", split_axis=0, concat_axis=0, tiled=True)

    def swap(weight):
        return lax.ppermute(lax.dynamic_index_in_dim(weight, 1 - index, 0, False), "tp", SWAP)

    in_far, up_far, out_far = swap(w_in), swap(w_up), swap(w_out)
    back = experts(core, message, w_in, w_up, w_out, in_far, up_far, out_far)
    parts = back.shape
    back = back.reshape(2 * parts[0], parts[1] // 2, MAIN, BLOCK)
    returned = lax.all_to_all(back, ("dp", "tp"), split_axis=0, concat_axis=0, tiled=True)
    attn_out = attention(query_latent, query_rope, cache_latent, cache_rope, lengths)
    gates = gate_matrix(routes, route_gates.T, dp_count)
    moe_out = combine(returned.reshape(parts), gates, attn_out)
    return (moe_out, attn_out)


def solution(mesh):
    placed = (
        P("dp", None),
        P("dp", None),
        P("dp", None),
        P("dp", None, "tp"),
        P("dp", None, "tp"),
        P("dp", "tp", None),
        P("dp", None, None),
        P("dp", None, None),
        P("dp", "tp", None),
        P("dp", None, "tp"),
        P("dp"),
    )
    return jax.shard_map(
        body,
        mesh=mesh,
        in_specs=placed,
        out_specs=(P("dp", "tp"), P("dp", None, None)),
        check_vma=False,
    )
```
